128 devices in a mesh: ctx: 16 (over y, x), head: 8 (over z, core).
Axes of the slice: x: 4, y: 4, z: 4, core: 2. Of those that a mesh axis runs over, the one named last changes fastest.
Arguments:
- routed_q: bfloat16 [8192, 1024], P('ctx', 'head'), may hold values from -16 to 16
- routed_k: bfloat16 [8192, 1024], P('ctx', 'head'), may hold values from -16 to 16
- routed_v: bfloat16 [8192, 1024], P('ctx', 'head'), may hold values from -6 to 6
- routed_grad: bfloat16 [8192, 1024], P('ctx', 'head'), may hold values from -6 to 6
- local_q: bfloat16 [8192, 1024], P('ctx', 'head'), may hold values from -16 to 16
- local_k: bfloat16 [8192, 1024], P('ctx', 'head'), may hold values from -16 to 16
- local_v: bfloat16 [8192, 1024], P('ctx', 'head'), may hold values from -6 to 6
- local_grad: bfloat16 [8192, 1024], P('ctx', 'head'), may hold values from -6 to 6
- clusters: int32 [8, 8192], P('head', 'ctx'), may hold values from 0 to 127, as said below
- cluster_slot: int32 [8, 128], P('head'), may hold values from 0 to 127, each once within a row
- rel_bias: float32 [128], replicated, may hold values from -4 to 4
Outputs:
- routed_out: bfloat16 [8192, 1024], P('ctx', 'head')
- routed_dq: bfloat16 [8192, 1024], P('ctx', 'head')
- routed_dk: bfloat16 [8192, 1024], P('ctx', 'head')
- routed_dv: bfloat16 [8192, 1024], P('ctx', 'head')
- centroids: float32 [8, 128, 128], P('head', 'ctx')
- local_out: bfloat16 [8192, 1024], P('ctx', 'head')
- local_dq: bfloat16 [8192, 1024], P('ctx', 'head')
- local_dk: bfloat16 [8192, 1024], P('ctx', 'head')
- local_dv: bfloat16 [8192, 1024], P('ctx', 'head')
- bias_grad: float32 [128], replicated
The draws below stay inside these ranges and needn't reach their ends.
Inputs may be any that keep to these rules, and one draw needn't show every extreme that they name: `clusters`: among the 512 positions of one index of ctx, at most 8 name the same cluster for one routed head; for every routed head one cluster is named exactly 8 times on every index of ctx.
All inputs are finite; a program needn't handle non-finite values.
Results may differ from the reference program's by a relative error of at most 0.0077.
Values may be sent and summed in bfloat16 or wider, within the bound.
A program may use at most 64 MiB of HBM per device.

```python
import jax
import jax.numpy as jnp
from jax import lax

HEAD_DIM = 128
ROUTED_HEADS = 8
LOCAL_HEADS = 8
WINDOW = 128
TOK_DEV = 512
SEQUENCE = 8192
CLUST_DEV = 8
CLUSTERS = 128
PER_SOURCE = 8
CAPACITY = 128
N_CTX = 16


def cluster_table(key):
    device_count = SEQUENCE // TOK_DEV
    pair_count = CLUSTERS // 2
    base_key = jax.random.fold_in(key, 7)
    key_division, key_labels, key_orders = jax.random.split(base_key, 3)
    division = jax.random.randint(key_division, (ROUTED_HEADS, device_count, pair_count), 0, PER_SOURCE + 1)
    division = division.at[:, :, 0].set(PER_SOURCE)
    position = jnp.arange(TOK_DEV, dtype=jnp.int32)
    pair_index = position // PER_SOURCE
    within = position % PER_SOURCE
    chosen = division[:, :, pair_index]
    labels = 2 * pair_index[None, None, :] + (within[None, None, :] >= chosen).astype(jnp.int32)
    relabel = jax.vmap(lambda sub_key: jax.random.permutation(sub_key, CLUSTERS))(jax.random.split(key_labels, ROUTED_HEADS)).astype(jnp.int32)
    labels = jax.vmap(lambda table, entries: table[entries])(relabel, labels)
    orders = jax.vmap(lambda sub_key: jax.random.permutation(sub_key, TOK_DEV))(jax.random.split(key_orders, ROUTED_HEADS * device_count))
    orders = orders.reshape(ROUTED_HEADS, device_count, TOK_DEV).astype(jnp.int32)
    labels = jnp.take_along_axis(labels, orders, axis=2)
    return labels.reshape(ROUTED_HEADS, SEQUENCE).astype(jnp.int32)


def routed_pair(key, which):
    gaussian = jax.random.truncated_normal(jax.random.fold_in(key, 20 + which), -6.0, 6.0, (SEQUENCE, ROUTED_HEADS, HEAD_DIM))
    return gaussian.reshape(SEQUENCE, ROUTED_HEADS * HEAD_DIM).astype(jnp.bfloat16)


def local_pair(key, which):
    gaussian = jax.random.truncated_normal(jax.random.fold_in(key, 40 + which), -6.0, 6.0, (SEQUENCE, LOCAL_HEADS, HEAD_DIM))
    return gaussian.reshape(SEQUENCE, LOCAL_HEADS * HEAD_DIM).astype(jnp.bfloat16)


def draw_routed_q(key, part):
    return routed_pair(key, 0)


def draw_routed_k(key, part):
    return routed_pair(key, 1)


def draw_local_q(key, part):
    return local_pair(key, 0)


def draw_local_k(key, part):
    return local_pair(key, 1)


def draw_clusters(key, part):
    return cluster_table(key)


def steps_of(rng, dims, cuts, least, top_value):
    def one(dim, parts):
        draws = jax.random.uniform(jax.random.fold_in(jax.random.fold_in(rng, 6), dim), (parts,), jnp.float32, least / len(cuts), top_value / len(cuts))
        return jnp.repeat(jnp.exp(draws), dims[dim] // parts).reshape((-1,) + (1,) * (len(dims) - dim - 1))

    level = one(*cuts[0])
    for cut in cuts[1:]:
        level = level * one(*cut)
    return level


def scatter_about(stream_key, dims, spread, reach, shards=(), kind=jnp.bfloat16):
    level = steps_of(stream_key, dims, shards, -0.22, 0.18) if shards else 1.0
    values = jax.random.normal(stream_key, dims, jnp.float32) * spread * level
    return jnp.minimum(jnp.maximum(values, -reach), reach).astype(kind)


def setup_inputs(seed: int = 0) -> dict:
    streams_of = jax.random.split(jax.random.key(seed), 12)
    return {
        "routed_q": draw_routed_q(jax.random.fold_in(streams_of[11], 71), 0),
        "routed_k": draw_routed_k(jax.random.fold_in(streams_of[11], 71), 0),
        "routed_v": scatter_about(streams_of[2], (SEQUENCE, ROUTED_HEADS * HEAD_DIM), 1.0, 6.0, ((0, 16), (1, 8))),
        "routed_grad": scatter_about(streams_of[3], (SEQUENCE, ROUTED_HEADS * HEAD_DIM), 1.0, 6.0, ((0, 16), (1, 8))),
        "local_q": draw_local_q(jax.random.fold_in(streams_of[11], 71), 0),
        "local_k": draw_local_k(jax.random.fold_in(streams_of[11], 71), 0),
        "local_v": scatter_about(streams_of[6], (SEQUENCE, LOCAL_HEADS * HEAD_DIM), 1.0, 6.0, ((0, 16), (1, 8))),
        "local_grad": scatter_about(streams_of[7], (SEQUENCE, LOCAL_HEADS * HEAD_DIM), 1.0, 6.0, ((0, 16), (1, 8))),
        "clusters": draw_clusters(jax.random.fold_in(streams_of[11], 71), 0),
        "cluster_slot": jax.vmap(lambda own: jax.random.permutation(own, CLUSTERS))(jax.random.split(streams_of[9], ROUTED_HEADS)).reshape((ROUTED_HEADS, CLUSTERS)).astype(jnp.int32),
        "rel_bias": scatter_about(streams_of[10], (WINDOW,), 1.0, 4.0, (), jnp.float32),
    }


NEG = -1e+30

def softmax_rows(query, keys, allowed, offset_bias):
    scaling = query.shape[-1] ** (-0.5)
    scores = jnp.einsum('bmd,bnd->bmn', query.astype(jnp.float32), keys.astype(jnp.float32)) * scaling + offset_bias
    scores = jnp.where(allowed, scores, NEG)
    row_max = lax.optimization_barrier(jnp.max(scores, axis=-1, keepdims=True))
    exponent = jnp.exp(scores - row_max)
    return exponent / lax.optimization_barrier(jnp.sum(exponent, axis=-1, keepdims=True))

def attend_all(query, keys, values, cotangent, allowed, offset_bias):
    attn_weights = softmax_rows(query, keys, allowed, offset_bias)
    weights_low = lax.optimization_barrier(attn_weights.astype(jnp.bfloat16)).astype(jnp.float32)
    values_wide = values.astype(jnp.float32)
    cot_wide = cotangent.astype(jnp.float32)
    output = jnp.einsum('bmn,bnd->bmd', weights_low, values_wide)
    weight_grad = jnp.einsum('bmd,bnd->bmn', cot_wide, values_wide)
    score_grad = attn_weights * (weight_grad - lax.optimization_barrier(jnp.sum(attn_weights * weight_grad, axis=-1, keepdims=True)))
    score_grad_low = lax.optimization_barrier(score_grad.astype(jnp.bfloat16)).astype(jnp.float32)
    scaling = query.shape[-1] ** (-0.5)
    query_grad = jnp.einsum('bmn,bnd->bmd', score_grad_low, keys.astype(jnp.float32)) * scaling
    keys_grad = jnp.einsum('bmn,bmd->bnd', score_grad_low, query.astype(jnp.float32)) * scaling
    values_grad = jnp.einsum('bmn,bmd->bnd', weights_low, cot_wide)
    return (output, query_grad, keys_grad, values_grad, score_grad)

def offset_table():
    row_index = jnp.arange(WINDOW, dtype=jnp.int32)[:, None]
    col_index = jnp.arange(2 * WINDOW, dtype=jnp.int32)[None, :]
    offset = WINDOW + row_index - col_index
    inside = (offset >= 0) & (offset < WINDOW)
    return (offset, inside)

def routed_head(inputs):
    query, keys, values, cotangent, cluster_ids, slots = inputs
    total = cluster_ids.shape[0]
    head_dim = query.shape[-1]
    sorted_pos = jnp.argsort(cluster_ids, stable=True).astype(jnp.int32)
    sorted_ids = cluster_ids[sorted_pos]
    counts = jnp.zeros((CLUSTERS,), jnp.int32).at[cluster_ids].add(1)
    starts = jnp.cumsum(counts) - counts
    rank_in = jnp.arange(total, dtype=jnp.int32) - starts[sorted_ids]
    destination = jnp.zeros((total,), jnp.int32).at[sorted_pos].set(sorted_ids * CAPACITY + rank_in)

    def pack(array):
        packed = jnp.zeros((CLUSTERS * CAPACITY, head_dim), array.dtype).at[destination].set(array)
        return packed.reshape(CLUST_DEV, N_CTX, CAPACITY, head_dim)
    live_slots = (jnp.arange(CAPACITY, dtype=jnp.int32)[None, :] < counts[:, None]).reshape(CLUST_DEV, N_CTX, CAPACITY)
    causal = jnp.arange(CAPACITY)[:, None] >= jnp.arange(CAPACITY)[None, :]
    diagonal = jnp.eye(CAPACITY, dtype=bool)

    def one_group(group):
        g_query, g_keys, g_values, g_cot, g_live = group
        allowed = g_live[:, None, :] & causal[None] | diagonal[None]
        output, query_grad, keys_grad, values_grad, unused = attend_all(g_query, g_keys, g_values, g_cot, allowed, 0.0)
        return (output.astype(jnp.bfloat16), query_grad.astype(jnp.bfloat16), keys_grad.astype(jnp.bfloat16), values_grad.astype(jnp.bfloat16))
    packed_keys = pack(keys)
    results = lax.map(one_group, (pack(query), packed_keys, pack(values), pack(cotangent), live_slots))
    back = [piece.reshape(CLUSTERS * CAPACITY, head_dim)[destination] for piece in results]
    key_sums = lax.optimization_barrier(jnp.sum(packed_keys.astype(jnp.float32).reshape(CLUSTERS, CAPACITY, head_dim), axis=1))
    normed = key_sums / jnp.sqrt(lax.optimization_barrier(jnp.mean(key_sums * key_sums, axis=-1, keepdims=True)) + 1e-06)
    placed = jnp.zeros_like(normed).at[slots].set(normed)
    return (back[0], back[1], back[2], back[3], placed)

def local_head(inputs, rel_bias):
    query, keys, values, cotangent = inputs
    total, head_dim = query.shape
    block_count = total // WINDOW

    def key_frames(array):
        extended = jnp.concatenate([jnp.zeros((WINDOW, head_dim), array.dtype), array], 0)
        return jnp.concatenate([extended[:-WINDOW].reshape(block_count, WINDOW, head_dim), extended[WINDOW:].reshape(block_count, WINDOW, head_dim)], 1)

    def fold_frames(array):
        earlier_half = array[:, :WINDOW].reshape(total, head_dim)
        later_half = array[:, WINDOW:].reshape(total, head_dim)
        return (jnp.pad(earlier_half, ((0, WINDOW), (0, 0))) + jnp.pad(later_half, ((WINDOW, 0), (0, 0))))[WINDOW:]
    offset, inside = offset_table()
    offset_bias = rel_bias[jnp.clip(offset, 0, WINDOW - 1)]
    key_pos = jnp.arange(block_count, dtype=jnp.int32)[:, None, None] * WINDOW - WINDOW + jnp.arange(2 * WINDOW, dtype=jnp.int32)[None, None, :]
    allowed = inside[None] & (key_pos >= 0)
    output, query_grad, keys_grad, values_grad, score_grad = attend_all(query.reshape(block_count, WINDOW, head_dim), key_frames(keys), key_frames(values), cotangent.reshape(block_count, WINDOW, head_dim), allowed, offset_bias)
    return (output.reshape(total, head_dim).astype(jnp.bfloat16), query_grad.reshape(total, head_dim).astype(jnp.bfloat16), fold_frames(keys_grad).astype(jnp.bfloat16), fold_frames(values_grad).astype(jnp.bfloat16), lax.optimization_barrier(jnp.sum(score_grad, axis=0)))

def reference(routed_q, routed_k, routed_v, routed_grad, local_q, local_k, local_v, local_grad, clusters, cluster_slot, rel_bias):

    def by_head(array):
        return array.reshape(SEQUENCE, -1, HEAD_DIM).transpose(1, 0, 2)

    def merge_heads(array):
        return array.transpose(1, 0, 2).reshape(SEQUENCE, -1)
    routed = lax.map(routed_head, (by_head(routed_q), by_head(routed_k), by_head(routed_v), by_head(routed_grad), clusters, cluster_slot))
    local = lax.map(lambda group: local_head(group, rel_bias), (by_head(local_q), by_head(local_k), by_head(local_v), by_head(local_grad)))
    offset, inside = offset_table()
    segment_ids = jnp.where(inside, offset, WINDOW).reshape(-1)
    bias_grad = jax.ops.segment_sum(lax.optimization_barrier(jnp.sum(local[4], axis=0)).reshape(-1), segment_ids, num_segments=WINDOW + 1)[:WINDOW]
    return (merge_heads(routed[0]), merge_heads(routed[1]), merge_heads(routed[2]), merge_heads(routed[3]), routed[4], merge_heads(local[0]), merge_heads(local[1]), merge_heads(local[2]), merge_heads(local[3]), bias_grad)
```

```python
import functools

import jax
import jax.numpy as jnp
from jax import lax
from jax.experimental import pallas as pl
from jax.experimental.pallas import tpu as pltpu
from jax.sharding import PartitionSpec as P

TOK = 512
DIM = 128
WINDOW = 128
N_CTX = 16
N_HEAD = 8
CHUNKS = 4
ROWS = 16
SPAN = N_CTX * ROWS
NEG = -1e30
EPSILON = 1e-06
SCALE = DIM ** (-0.5)
F32 = jnp.float32
BF16 = jnp.bfloat16
I32 = jnp.int32
MESH = pl.DeviceIdType.MESH


def iota(shape, dim):
    return lax.broadcasted_iota(I32, shape, dim)


def mm(a, b):
    return jnp.dot(a, b, preferred_element_type=F32)


def mm_nt(a, b):
    return lax.dot_general(a, b, (((1,), (1,)), ((), ())), preferred_element_type=F32)


def mm_tn(a, b):
    return lax.dot_general(a, b, (((0,), (0,)), ((), ())), preferred_element_type=F32)


def attention(q, k, v, g, mask):
    scores = mm_nt(q, k) * SCALE + mask
    top = jnp.max(scores, axis=-1, keepdims=True)
    e = jnp.exp(scores - top)
    p = e / jnp.sum(e, axis=-1, keepdims=True)
    p_low = p.astype(BF16)
    dp = mm_nt(g, v)
    ds = p * (dp - jnp.sum(p * dp, axis=-1, keepdims=True))
    ds_low = ds.astype(BF16)
    out = mm(p_low, v)
    dq = mm(ds_low, k) * SCALE
    dk = mm_tn(ds_low, q) * SCALE
    dv = mm_tn(p_low, g)
    return out, dq, dk, dv, ds


def kernel(
    rq, rk, rv, rg, lq, lk, lv, lg, cl, slot, rb,
    o_ro, o_rdq, o_rdk, o_rdv, o_cent, o_lo, o_ldq, o_ldk, o_ldv, o_bias,
    tok, wq, wk, wv, wg, cl_v, slot_v, rb_v,
    send, recv, ret_send, ret_recv, halo, grad_send, grad_recv,
    cnt_send, cnt_recv, bias_a, bias_a_recv, bias_b, bias_b_recv,
    flat_v, back_hot, live_v, mask_v, wbias, acc, wacc,
    ro_v, wo_v, cent_v, bias_v, bias_sum,
    in_sem, out_sem, send_sem, recv_sem, rsend_sem, rrecv_sem,
    halo_ssem, halo_rsem, grad_ssem, grad_rsem, small_ssem, small_rsem, self_sem,
):
    me = lax.axis_index("ctx")
    my_head = lax.axis_index("head")
    my_x = lax.rem(me, 4)
    my_y = lax.div(me, 4)
    ahead = lax.rem(me + 1, N_CTX)
    behind = lax.rem(me + N_CTX - 1, N_CTX)

    def peer(step):
        px = lax.rem(my_x + lax.rem(step, 4), 4)
        py = lax.rem(my_y + lax.div(step, 4), 4)
        return py * 4 + px

    def fetch(src, dst, i):
        copy = pltpu.make_async_copy(src, dst, in_sem.at[i])
        copy.start()
        return copy

    small_in = [fetch(cl, cl_v, 0), fetch(slot, slot_v, 1), fetch(rb, rb_v, 2)]
    routed_in = [
        fetch(src, tok.at[:, pl.ds(i * DIM, DIM)], 3 + i) for i, src in enumerate((rq, rk, rv, rg))
    ]
    local_in = [fetch(src, dst, 7 + i) for i, (src, dst) in enumerate(((lk, wk), (lv, wv), (lq, wq), (lg, wg)))]

    barrier = pltpu.get_barrier_semaphore()

    @pl.loop(1, N_CTX)
    def _(step):
        pl.semaphore_signal(barrier, inc=1, device_id={"ctx": peer(step)}, device_id_type=MESH)

    @pl.loop(1, N_HEAD)
    def _(step):
        pl.semaphore_signal(
            barrier, inc=1, device_id={"head": lax.rem(my_head + step, N_HEAD)}, device_id_type=MESH
        )

    for copy in small_in:
        copy.wait()
    cluster_rows = iota((DIM, TOK), 0)
    named = (cl_v[...] == cluster_rows).astype(F32).astype(BF16)
    slots16 = jnp.broadcast_to(slot_v[...].astype(F32), (16, DIM)).astype(BF16)
    slot_of = mm(slots16, named)[0:1].astype(I32)
    in_slot = slot_of == cluster_rows
    placed = in_slot.astype(F32).astype(BF16)
    upto = (iota((TOK, TOK), 0) <= iota((TOK, TOK), 1)).astype(F32).astype(BF16)
    ranks = mm(placed, upto)
    rank = jnp.sum(jnp.where(in_slot, ranks, 0.0), axis=0, keepdims=True).astype(I32) - 1
    flat = (
        ((slot_of >> 1) & 3) * SPAN + (slot_of >> 3) * ROWS + (slot_of & 1) * 8 + rank
    )
    flat_v[...] = flat
    cnt_send[...] = mm_nt(jnp.ones((16, TOK), BF16), placed)[0:1]

    for copy in routed_in:
        copy.wait()

    def pack(c):
        hot = (flat_v[...] == iota((SPAN, TOK), 0) + c * SPAN).astype(F32).astype(BF16)
        rows = mm(hot, tok[...]).astype(BF16)
        for a in range(4):
            send[c, :, a] = rows[:, a * DIM : (a + 1) * DIM].reshape(N_CTX, ROWS, DIM)

    pl.semaphore_wait(barrier, N_CTX - 1 + N_HEAD - 1)

    for copy in local_in[:2]:
        copy.wait()
    for i, src in enumerate((wk, wv)):
        pltpu.make_async_remote_copy(
            src.at[pl.ds(TOK - WINDOW, WINDOW)], halo.at[i], halo_ssem.at[i], halo_rsem.at[i],
            device_id={"ctx": ahead}, device_id_type=MESH,
        ).start()

    @pl.loop(1, N_CTX)
    def _(step):
        pltpu.make_async_remote_copy(
            cnt_send, cnt_recv.at[me], small_ssem.at[0], small_rsem.at[0],
            device_id={"ctx": peer(step)}, device_id_type=MESH,
        ).start()

    own_count = pltpu.make_async_copy(cnt_send, cnt_recv.at[me], self_sem.at[0])
    own_count.start()

    @pl.loop(0, CHUNKS)
    def _(c):
        pack(c)

        @pl.loop(1, N_CTX)
        def _(step):
            to = peer(step)
            pltpu.make_async_remote_copy(
                send.at[c, to], recv.at[c, me], send_sem.at[c], recv_sem.at[c],
                device_id={"ctx": to}, device_id_type=MESH,
            ).start()

        pltpu.make_async_copy(send.at[c, me], recv.at[c, me], recv_sem.at[c]).start()

    back_hot[...] = jnp.zeros_like(back_hot)
    flat_col = jnp.transpose(jnp.broadcast_to(flat.astype(F32), (8, TOK)))[:, 0:1].astype(I32)

    @pl.loop(0, CHUNKS)
    def _(c):
        back_hot[c] = (flat_col == iota((TOK, SPAN), 1) + c * SPAN).astype(F32).astype(BF16)

    row_i = iota((WINDOW, 2 * WINDOW), 0)
    col_i = iota((WINDOW, 2 * WINDOW), 1)
    bias_col = jnp.sum(
        jnp.where(iota((DIM, DIM), 0) == iota((DIM, DIM), 1), rb_v[...], 0.0), axis=1, keepdims=True
    )
    spread = jnp.sum(jnp.where(row_i == WINDOW - col_i, bias_col, 0.0), axis=0, keepdims=True)
    spread = jnp.broadcast_to(spread, (WINDOW, 2 * WINDOW))
    for b in range(7):
        spread = jnp.where((row_i >> b) & 1 == 1, pltpu.roll(spread, 1 << b, 1), spread)
    offset = WINDOW + row_i - col_i
    wbias[...] = jnp.where((offset >= 0) & (offset < WINDOW), spread, NEG)

    for copy in local_in[2:]:
        copy.wait()

    def local_block(b, k, v, mask):
        rows = pl.ds(b * WINDOW, WINDOW)
        out, dq, dk, dv, ds = attention(wq[rows], k, v, wg[rows], mask)
        wo_v[0, rows] = out.astype(BF16)
        wo_v[1, rows] = dq.astype(BF16)
        return dk, dv, ds

    wacc[...] = jnp.zeros_like(wacc)
    bias_v[...] = jnp.zeros_like(bias_v)

    @pl.loop(1, 4)
    def _(b):
        at = pl.multiple_of((b - 1) * WINDOW, WINDOW)
        frame = pl.ds(at, 2 * WINDOW)
        dk, dv, ds = local_block(b, wk[frame], wv[frame], wbias[...])
        wacc[0, frame] += dk
        wacc[1, frame] += dv
        bias_v[...] += ds

    for i in range(2):
        pltpu.make_async_remote_copy(
            wk.at[pl.ds(0, WINDOW)], halo.at[i], halo_ssem.at[i], halo_rsem.at[i],
            device_id={"ctx": ahead}, device_id_type=MESH,
        ).wait_recv()
    first = jnp.where((col_i < WINDOW) & (me == 0), NEG, wbias[...])
    own = pl.ds(0, WINDOW)
    dk, dv, ds = local_block(
        0,
        jnp.concatenate([halo[0], wk[own]], axis=0),
        jnp.concatenate([halo[1], wv[own]], axis=0),
        first,
    )
    for i, d in enumerate((dk, dv)):
        grad_send[i] = d[:WINDOW].astype(BF16)
        wacc[i, own] += d[WINDOW:]
        pltpu.make_async_remote_copy(
            grad_send.at[i], grad_recv.at[i], grad_ssem.at[i], grad_rsem.at[i],
            device_id={"ctx": behind}, device_id_type=MESH,
        ).start()

    total = bias_v[...] + ds
    for b in range(7):
        total = jnp.where((row_i >> b) & 1 == 1, pltpu.roll(total, 2 * WINDOW - (1 << b), 1), total)
    by_col = jnp.sum(total, axis=0, keepdims=True)
    square = (2 * WINDOW, 2 * WINDOW)
    by_row = jnp.sum(jnp.where(iota(square, 0) == iota(square, 1), by_col, 0.0), axis=1, keepdims=True)
    tall = (2 * WINDOW, WINDOW)
    bias_a[...] = jnp.sum(
        jnp.where(iota(tall, 0) == WINDOW - iota(tall, 1), by_row, 0.0), axis=0, keepdims=True
    )

    @pl.loop(1, N_CTX)
    def _(step):
        pltpu.make_async_remote_copy(
            bias_a, bias_a_recv.at[me], small_ssem.at[1], small_rsem.at[1],
            device_id={"ctx": peer(step)}, device_id_type=MESH,
        ).start()

    own_bias = pltpu.make_async_copy(bias_a, bias_a_recv.at[me], self_sem.at[1])
    own_bias.start()

    own_count.wait()
    pltpu.make_async_copy(
        cnt_recv.at[pl.ds(0, N_CTX - 1)], cnt_recv.at[pl.ds(0, N_CTX - 1)], small_rsem.at[0]
    ).wait()
    counts = jnp.concatenate([cnt_recv[s] for s in range(N_CTX)], axis=0).astype(BF16)
    wide = (DIM, CHUNKS * SPAN)
    j = iota(wide, 1)
    pick = iota(wide, 0) == me * 8 + (j >> 8) * 2 + ((j >> 3) & 1)
    picked = mm(counts, pick.astype(F32).astype(BF16))
    j = iota((N_CTX, CHUNKS * SPAN), 1)
    held = jnp.sum(
        jnp.where(iota((N_CTX, CHUNKS * SPAN), 0) == ((j >> 4) & 15), picked, 0.0), axis=0, keepdims=True
    )
    live = jnp.where((iota((1, CHUNKS * SPAN), 1) & 7).astype(F32) < held, 0.0, NEG)
    for c in range(CHUNKS):
        live_v[c] = live[:, c * SPAN : (c + 1) * SPAN]
    span = (SPAN, SPAN)
    si, sj = iota(span, 0), iota(span, 1)
    mask_v[...] = jnp.where((((si ^ sj) & 8) == 0) & (sj <= si), 0.0, NEG)

    @pl.loop(0, CHUNKS)
    def _(c):
        pltpu.make_async_copy(recv.at[c], recv.at[c], recv_sem.at[c]).wait()
        q, k, v, g = (recv[c, :, a].reshape(SPAN, DIM) for a in range(4))
        out, dq, dk, dv, _ = attention(q, k, v, g, mask_v[...] + live_v[c])
        for a, r in enumerate((out, dq, dk, dv)):
            ret_send[c, :, a] = r.astype(BF16).reshape(N_CTX, ROWS, DIM)

        @pl.loop(1, N_CTX)
        def _(step):
            to = peer(step)
            pltpu.make_async_remote_copy(
                ret_send.at[c, to], ret_recv.at[c, me], rsend_sem.at[c], rrecv_sem.at[c],
                device_id={"ctx": to}, device_id_type=MESH,
            ).start()

        pltpu.make_async_copy(ret_send.at[c, me], ret_recv.at[c, me], rrecv_sem.at[c]).start()
        pick = (((iota((16, SPAN), 1) >> 3) & 1) == iota((16, SPAN), 0)).astype(F32).astype(BF16)
        sums = mm(pick, k)[0:2]
        cent_v[c] = sums / jnp.sqrt(jnp.mean(sums * sums, axis=-1, keepdims=True) + EPSILON)

    own_bias.wait()
    pltpu.make_async_copy(
        bias_a_recv.at[pl.ds(0, N_CTX - 1)], bias_a_recv.at[pl.ds(0, N_CTX - 1)], small_rsem.at[1]
    ).wait()
    bias_b[...] = jnp.sum(bias_a_recv[...], axis=0)

    @pl.loop(1, N_HEAD)
    def _(step):
        pltpu.make_async_remote_copy(
            bias_b, bias_b_recv.at[my_head], small_ssem.at[2], small_rsem.at[2],
            device_id={"head": lax.rem(my_head + step, N_HEAD)}, device_id_type=MESH,
        ).start()

    own_sum = pltpu.make_async_copy(bias_b, bias_b_recv.at[my_head], self_sem.at[2])
    own_sum.start()

    for i in range(2):
        pltpu.make_async_remote_copy(
            grad_send.at[i], grad_recv.at[i], grad_ssem.at[i], grad_rsem.at[i],
            device_id={"ctx": behind}, device_id_type=MESH,
        ).wait_recv()
        wacc[i, pl.ds(TOK - WINDOW, WINDOW)] += grad_recv[i].astype(F32)
        wo_v[2 + i] = wacc[i].astype(BF16)
    outs = []

    def put(src, dst, i):
        copy = pltpu.make_async_copy(src, dst, out_sem.at[i])
        copy.start()
        outs.append(copy)

    for i, dst in enumerate((o_lo, o_ldq, o_ldk, o_ldv)):
        put(wo_v.at[i], dst, i)
    for c in range(CHUNKS):
        put(cent_v.at[c], o_cent.at[pl.ds(2 * c, 2)], 4 + c)

    own_sum.wait()
    pltpu.make_async_copy(
        bias_b_recv.at[pl.ds(0, N_HEAD - 1)], bias_b_recv.at[pl.ds(0, N_HEAD - 1)], small_rsem.at[2]
    ).wait()
    bias_sum[...] = jnp.sum(bias_b_recv[...], axis=0)
    put(bias_sum, o_bias, 8)

    acc[...] = jnp.zeros_like(acc)

    @pl.loop(0, CHUNKS)
    def _(c):
        pltpu.make_async_copy(ret_recv.at[c], ret_recv.at[c], rrecv_sem.at[c]).wait()
        rows = jnp.concatenate([ret_recv[c, :, a].reshape(SPAN, DIM) for a in range(4)], axis=1)
        acc[...] += mm(back_hot[c], rows)

    for a, dst in enumerate((o_ro, o_rdq, o_rdk, o_rdv)):
        ro_v[a] = acc[:, a * DIM : (a + 1) * DIM].astype(BF16)
        put(ro_v.at[a], dst, 9 + a)

    for c in range(CHUNKS):
        part = send.at[c, pl.ds(0, N_CTX - 1)]
        pltpu.make_async_copy(part, part, send_sem.at[c]).wait()
        part = ret_send.at[c, pl.ds(0, N_CTX - 1)]
        pltpu.make_async_copy(part, part, rsend_sem.at[c]).wait()
    for i in range(2):
        pltpu.make_async_copy(halo.at[i], halo.at[i], halo_ssem.at[i]).wait()
        pltpu.make_async_copy(grad_send.at[i], grad_send.at[i], grad_ssem.at[i]).wait()
    for i, n in enumerate((N_CTX, N_CTX, N_HEAD)):
        part = cnt_recv.at[pl.ds(0, n - 1)]
        pltpu.make_async_copy(part, part, small_ssem.at[i]).wait()
    for copy in outs:
        copy.wait()


def shards(rq, rk, rv, rg, lq, lk, lv, lg, clusters, cluster_slot, rel_bias):
    token_out = jax.ShapeDtypeStruct((TOK, DIM), BF16)
    vm = pltpu.VMEM
    dma = pltpu.SemaphoreType.DMA
    scratch = [
        vm((TOK, 4 * DIM), BF16),
        vm((TOK, DIM), BF16), vm((TOK, DIM), BF16), vm((TOK, DIM), BF16), vm((TOK, DIM), BF16),
        vm((1, TOK), I32), vm((1, DIM), I32), vm((1, DIM), F32),
        vm((CHUNKS, N_CTX, 4, ROWS, DIM), BF16), vm((CHUNKS, N_CTX, 4, ROWS, DIM), BF16),
        vm((CHUNKS, N_CTX, 4, ROWS, DIM), BF16), vm((CHUNKS, N_CTX, 4, ROWS, DIM), BF16),
        vm((2, WINDOW, DIM), BF16), vm((2, WINDOW, DIM), BF16), vm((2, WINDOW, DIM), BF16),
        vm((1, DIM), F32), vm((N_CTX, 1, DIM), F32),
        vm((1, DIM), F32), vm((N_CTX, 1, DIM), F32),
        vm((1, DIM), F32), vm((N_HEAD, 1, DIM), F32),
        vm((1, TOK), I32), vm((CHUNKS, TOK, SPAN), BF16), vm((CHUNKS, 1, SPAN), F32),
        vm((SPAN, SPAN), F32), vm((WINDOW, 2 * WINDOW), F32), vm((TOK, 4 * DIM), F32),
        vm((2, TOK, DIM), F32),
        vm((4, TOK, DIM), BF16), vm((4, TOK, DIM), BF16), vm((CHUNKS, 2, DIM), F32),
        vm((WINDOW, 2 * WINDOW), F32), vm((1, DIM), F32),
        dma((11,)), dma((13,)),
        dma((CHUNKS,)), dma((CHUNKS,)), dma((CHUNKS,)), dma((CHUNKS,)),
        dma((2,)), dma((2,)), dma((2,)), dma((2,)), dma((3,)), dma((3,)), dma((3,)),
    ]
    anywhere = pl.BlockSpec(memory_space=pl.ANY)
    outs = pl.pallas_call(
        kernel,
        out_shape=[token_out] * 4
        + [jax.ShapeDtypeStruct((8, DIM), F32)]
        + [token_out] * 4
        + [jax.ShapeDtypeStruct((1, DIM), F32)],
        in_specs=[anywhere] * 11,
        out_specs=[anywhere] * 10,
        scratch_shapes=scratch,
        compiler_params=pltpu.CompilerParams(
            collective_id=0, has_side_effects=True, vmem_limit_bytes=40 * 1024 * 1024
        ),
        name="routing",
    )(rq, rk, rv, rg, lq, lk, lv, lg, clusters, cluster_slot, rel_bias.reshape(1, DIM))
    ro, rdq, rdk, rdv, cent, lo, ldq, ldk, ldv, bias = outs
    return (
        ro, rdq, rdk, rdv, cent.reshape(1, 8, DIM), lo, ldq, ldk, ldv, bias.reshape(DIM),
    )


def solution(mesh):
    tokens = P("ctx", "head")
    return jax.shard_map(
        shards,
        mesh=mesh,
        in_specs=(tokens,) * 8 + (P("head", "ctx"), P("head", None), P()),
        out_specs=(tokens,) * 4 + (P("head", "ctx", None),) + (tokens,) * 4 + (P(),),
        check_vma=False,
    )
```

```python
import functools

import jax
import jax.numpy as jnp
from jax import lax
from jax.experimental import pallas as pl
from jax.experimental.pallas import tpu as pltpu
from jax.sharding import PartitionSpec as P

TOK = 512
DIM = 128
WINDOW = 128
N_CTX = 16
N_HEAD = 8
CHUNKS = 4
ROWS = 16
SPAN = N_CTX * ROWS
NEG = -1e30
EPSILON = 1e-06
VMEM_GRANT = 54140 * 1024
SCALE = DIM ** (-0.5)
F32 = jnp.float32
BF16 = jnp.bfloat16
I32 = jnp.int32
MESH = pl.DeviceIdType.MESH


def iota(shape, dim):
    return lax.broadcasted_iota(I32, shape, dim)


def mm(a, b):
    return jnp.dot(a, b, preferred_element_type=F32)


def mm_nt(a, b):
    return lax.dot_general(a, b, (((1,), (1,)), ((), ())), preferred_element_type=F32)


def mm_tn(a, b):
    return lax.dot_general(a, b, (((0,), (0,)), ((), ())), preferred_element_type=F32)


def attention(q, k, v, g, mask):
    scores = mm_nt(q, k) * SCALE + mask
    top = jnp.max(scores, axis=-1, keepdims=True)
    e = jnp.exp(scores - top)
    p = e / jnp.sum(e, axis=-1, keepdims=True)
    p_low = p.astype(BF16)
    dp = mm_nt(g, v)
    ds = p * (dp - jnp.sum(p * dp, axis=-1, keepdims=True))
    ds_low = ds.astype(BF16)
    out = mm(p_low, v)
    dq = mm(ds_low, k) * SCALE
    dk = mm_tn(ds_low, q) * SCALE
    dv = mm_tn(p_low, g)
    return out, dq, dk, dv, ds


def kernel(
    rq, rk, rv, rg, lq, lk, lv, lg, cl, slot, rb,
    o_ro, o_rdq, o_rdk, o_rdv, o_lo, o_ldq, o_ldk, o_ldv, o_cent, o_bias,
    tok, wq, wk, wv, wg,
    send, recv, ret_send, ret_recv, halo, grad_send, grad_recv,
    cnt_send, cnt_recv, bias_a, bias_a_recv, bias_b, bias_b_recv,
    flat_v, back_hot, live_v, mask_v, wbias, acc, wacc,
    bias_v,
    in_sem, send_sem, recv_sem, rsend_sem, rrecv_sem,
    halo_ssem, halo_rsem, grad_ssem, grad_rsem, small_ssem, small_rsem, self_sem,
):
    me = lax.axis_index("ctx")
    my_head = lax.axis_index("head")
    my_x = lax.rem(me, 4)
    my_y = lax.div(me, 4)
    ahead = lax.rem(me + 1, N_CTX)
    behind = lax.rem(me + N_CTX - 1, N_CTX)

    def peer(step):
        px = lax.rem(my_x + lax.rem(step, 4), 4)
        py = lax.rem(my_y + lax.div(step, 4), 4)
        return py * 4 + px

    def fetch(src, dst, i):
        copy = pltpu.make_async_copy(src, dst, in_sem.at[i])
        copy.start()
        return copy

    routed_in = [
        fetch(src, tok.at[:, pl.ds(i * DIM, DIM)], i) for i, src in enumerate((rq, rk, rv, rg))
    ]
    local_in = [fetch(src, dst, 4 + i) for i, (src, dst) in enumerate(((lk, wk), (lv, wv), (lq, wq), (lg, wg)))]

    barrier = pltpu.get_barrier_semaphore()

    @pl.loop(1, N_CTX)
    def _(step):
        pl.semaphore_signal(barrier, inc=1, device_id={"ctx": peer(step)}, device_id_type=MESH)

    @pl.loop(1, N_HEAD)
    def _(step):
        pl.semaphore_signal(
            barrier, inc=1, device_id={"head": lax.rem(my_head + step, N_HEAD)}, device_id_type=MESH
        )

    cluster_rows = iota((DIM, TOK), 0)
    named = (cl[...] == cluster_rows).astype(F32).astype(BF16)
    slots16 = jnp.broadcast_to(slot[...].astype(F32), (16, DIM)).astype(BF16)
    slot_of = mm(slots16, named)[0:1].astype(I32)
    in_slot = slot_of == cluster_rows
    placed = in_slot.astype(F32).astype(BF16)
    upto = (iota((TOK, TOK), 0) <= iota((TOK, TOK), 1)).astype(F32).astype(BF16)
    ranks = mm(placed, upto)
    rank = jnp.sum(jnp.where(in_slot, ranks, 0.0), axis=0, keepdims=True).astype(I32) - 1
    flat = (
        ((slot_of >> 1) & 3) * SPAN + (slot_of >> 3) * ROWS + (slot_of & 1) * 8 + rank
    )
    flat_v[...] = flat
    cnt_send[...] = mm_nt(jnp.ones((16, TOK), BF16), placed)[0:1]

    for copy in routed_in:
        copy.wait()

    def pack(c):
        hot = (flat_v[...] == iota((SPAN, TOK), 0) + c * SPAN).astype(F32).astype(BF16)
        rows = mm(hot, tok[...]).astype(BF16)
        for a in range(4):
            send[c, :, a] = rows[:, a * DIM : (a + 1) * DIM].reshape(N_CTX, ROWS, DIM)

    pl.semaphore_wait(barrier, N_CTX - 1 + N_HEAD - 1)

    for copy in local_in[:2]:
        copy.wait()
    for i, src in enumerate((wk, wv)):
        pltpu.make_async_remote_copy(
            src.at[pl.ds(TOK - WINDOW, WINDOW)], halo.at[i], halo_ssem.at[i], halo_rsem.at[i],
            device_id={"ctx": ahead}, device_id_type=MESH,
        ).start()

    @pl.loop(1, N_CTX)
    def _(step):
        pltpu.make_async_remote_copy(
            cnt_send, cnt_recv.at[me], small_ssem.at[0], small_rsem.at[0],
            device_id={"ctx": peer(step)}, device_id_type=MESH,
        ).start()

    own_count = pltpu.make_async_copy(cnt_send, cnt_recv.at[me], self_sem.at[0])
    own_count.start()

    @pl.loop(0, CHUNKS)
    def _(c):
        pack(c)

        @pl.loop(1, N_CTX)
        def _(step):
            to = peer(step)
            pltpu.make_async_remote_copy(
                send.at[c, to], recv.at[c, me], send_sem.at[c], recv_sem.at[c],
                device_id={"ctx": to}, device_id_type=MESH,
            ).start()

        pltpu.make_async_copy(send.at[c, me], recv.at[c, me], recv_sem.at[c]).start()

    back_hot[...] = jnp.zeros_like(back_hot)
    flat_col = jnp.transpose(jnp.broadcast_to(flat.astype(F32), (8, TOK)))[:, 0:1].astype(I32)

    @pl.loop(0, CHUNKS)
    def _(c):
        back_hot[c] = (flat_col == iota((TOK, SPAN), 1) + c * SPAN).astype(F32).astype(BF16)

    row_i = iota((WINDOW, 2 * WINDOW), 0)
    col_i = iota((WINDOW, 2 * WINDOW), 1)
    bias_col = jnp.sum(
        jnp.where(iota((DIM, DIM), 0) == iota((DIM, DIM), 1), rb[...], 0.0), axis=1, keepdims=True
    )
    spread = jnp.sum(jnp.where(row_i == WINDOW - col_i, bias_col, 0.0), axis=0, keepdims=True)
    spread = jnp.broadcast_to(spread, (WINDOW, 2 * WINDOW))
    for b in range(7):
        spread = jnp.where((row_i >> b) & 1 == 1, pltpu.roll(spread, 1 << b, 1), spread)
    offset = WINDOW + row_i - col_i
    wbias[...] = jnp.where((offset >= 0) & (offset < WINDOW), spread, NEG)

    for copy in local_in[2:]:
        copy.wait()

    def local_block(b, k, v, mask):
        rows = pl.ds(b * WINDOW, WINDOW)
        out, dq, dk, dv, ds = attention(wq[rows], k, v, wg[rows], mask)
        o_lo[rows] = out.astype(BF16)
        o_ldq[rows] = dq.astype(BF16)
        return dk, dv, ds

    wacc[...] = jnp.zeros_like(wacc)
    bias_v[...] = jnp.zeros_like(bias_v)

    @pl.loop(1, 4)
    def _(b):
        at = pl.multiple_of((b - 1) * WINDOW, WINDOW)
        frame = pl.ds(at, 2 * WINDOW)
        dk, dv, ds = local_block(b, wk[frame], wv[frame], wbias[...])
        wacc[0, frame] += dk
        wacc[1, frame] += dv
        bias_v[...] += ds

    for i in range(2):
        pltpu.make_async_remote_copy(
            wk.at[pl.ds(0, WINDOW)], halo.at[i], halo_ssem.at[i], halo_rsem.at[i],
            device_id={"ctx": ahead}, device_id_type=MESH,
        ).wait_recv()
    first = jnp.where((col_i < WINDOW) & (me == 0), NEG, wbias[...])
    own = pl.ds(0, WINDOW)
    dk, dv, ds = local_block(
        0,
        jnp.concatenate([halo[0], wk[own]], axis=0),
        jnp.concatenate([halo[1], wv[own]], axis=0),
        first,
    )
    for i, d in enumerate((dk, dv)):
        grad_send[i] = d[:WINDOW].astype(BF16)
        wacc[i, own] += d[WINDOW:]
        pltpu.make_async_remote_copy(
            grad_send.at[i], grad_recv.at[i], grad_ssem.at[i], grad_rsem.at[i],
            device_id={"ctx": behind}, device_id_type=MESH,
        ).start()

    total = bias_v[...] + ds
    for b in range(7):
        total = jnp.where((row_i >> b) & 1 == 1, pltpu.roll(total, 2 * WINDOW - (1 << b), 1), total)
    by_col = jnp.sum(total, axis=0, keepdims=True)
    square = (2 * WINDOW, 2 * WINDOW)
    by_row = jnp.sum(jnp.where(iota(square, 0) == iota(square, 1), by_col, 0.0), axis=1, keepdims=True)
    tall = (2 * WINDOW, WINDOW)
    bias_a[...] = jnp.sum(
        jnp.where(iota(tall, 0) == WINDOW - iota(tall, 1), by_row, 0.0), axis=0, keepdims=True
    )

    @pl.loop(1, N_CTX)
    def _(step):
        pltpu.make_async_remote_copy(
            bias_a, bias_a_recv.at[me], small_ssem.at[1], small_rsem.at[1],
            device_id={"ctx": peer(step)}, device_id_type=MESH,
        ).start()

    own_bias = pltpu.make_async_copy(bias_a, bias_a_recv.at[me], self_sem.at[1])
    own_bias.start()

    own_count.wait()
    pltpu.make_async_copy(
        cnt_recv.at[pl.ds(0, N_CTX - 1)], cnt_recv.at[pl.ds(0, N_CTX - 1)], small_rsem.at[0]
    ).wait()
    counts = jnp.concatenate([cnt_recv[s] for s in range(N_CTX)], axis=0).astype(BF16)
    wide = (DIM, CHUNKS * SPAN)
    j = iota(wide, 1)
    pick = iota(wide, 0) == me * 8 + (j >> 8) * 2 + ((j >> 3) & 1)
    picked = mm(counts, pick.astype(F32).astype(BF16))
    j = iota((N_CTX, CHUNKS * SPAN), 1)
    held = jnp.sum(
        jnp.where(iota((N_CTX, CHUNKS * SPAN), 0) == ((j >> 4) & 15), picked, 0.0), axis=0, keepdims=True
    )
    live = jnp.where((iota((1, CHUNKS * SPAN), 1) & 7).astype(F32) < held, 0.0, NEG)
    for c in range(CHUNKS):
        live_v[c] = live[:, c * SPAN : (c + 1) * SPAN]
    span = (SPAN, SPAN)
    si, sj = iota(span, 0), iota(span, 1)
    mask_v[...] = jnp.where((((si ^ sj) & 8) == 0) & (sj <= si), 0.0, NEG)

    @pl.loop(0, CHUNKS)
    def _(c):
        pltpu.make_async_copy(recv.at[c], recv.at[c], recv_sem.at[c]).wait()
        q, k, v, g = (recv[c, :, a].reshape(SPAN, DIM) for a in range(4))
        out, dq, dk, dv, _ = attention(q, k, v, g, mask_v[...] + live_v[c])
        for a, r in enumerate((out, dq, dk, dv)):
            ret_send[c, :, a] = r.astype(BF16).reshape(N_CTX, ROWS, DIM)

        @pl.loop(1, N_CTX)
        def _(step):
            to = peer(step)
            pltpu.make_async_remote_copy(
                ret_send.at[c, to], ret_recv.at[c, me], rsend_sem.at[c], rrecv_sem.at[c],
                device_id={"ctx": to}, device_id_type=MESH,
            ).start()

        pltpu.make_async_copy(ret_send.at[c, me], ret_recv.at[c, me], rrecv_sem.at[c]).start()
        pick = (((iota((16, SPAN), 1) >> 3) & 1) == iota((16, SPAN), 0)).astype(F32).astype(BF16)
        sums = mm(pick, k)[0:2]
        o_cent[c] = sums / jnp.sqrt(jnp.mean(sums * sums, axis=-1, keepdims=True) + EPSILON)

    own_bias.wait()
    pltpu.make_async_copy(
        bias_a_recv.at[pl.ds(0, N_CTX - 1)], bias_a_recv.at[pl.ds(0, N_CTX - 1)], small_rsem.at[1]
    ).wait()
    bias_b[...] = jnp.sum(bias_a_recv[...], axis=0)

    @pl.loop(1, N_HEAD)
    def _(step):
        pltpu.make_async_remote_copy(
            bias_b, bias_b_recv.at[my_head], small_ssem.at[2], small_rsem.at[2],
            device_id={"head": lax.rem(my_head + step, N_HEAD)}, device_id_type=MESH,
        ).start()

    own_sum = pltpu.make_async_copy(bias_b, bias_b_recv.at[my_head], self_sem.at[2])
    own_sum.start()

    for i in range(2):
        pltpu.make_async_remote_copy(
            grad_send.at[i], grad_recv.at[i], grad_ssem.at[i], grad_rsem.at[i],
            device_id={"ctx": behind}, device_id_type=MESH,
        ).wait_recv()
        wacc[i, pl.ds(TOK - WINDOW, WINDOW)] += grad_recv[i].astype(F32)
        (o_ldk, o_ldv)[i][...] = wacc[i].astype(BF16)
    own_sum.wait()
    pltpu.make_async_copy(
        bias_b_recv.at[pl.ds(0, N_HEAD - 1)], bias_b_recv.at[pl.ds(0, N_HEAD - 1)], small_rsem.at[2]
    ).wait()
    o_bias[...] = jnp.sum(bias_b_recv[...], axis=0)

    acc[...] = jnp.zeros_like(acc)

    @pl.loop(0, CHUNKS)
    def _(c):
        pltpu.make_async_copy(ret_recv.at[c], ret_recv.at[c], rrecv_sem.at[c]).wait()
        rows = jnp.concatenate([ret_recv[c, :, a].reshape(SPAN, DIM) for a in range(4)], axis=1)
        acc[...] += mm(back_hot[c], rows)

    for a, dst in enumerate((o_ro, o_rdq, o_rdk, o_rdv)):
        dst[...] = acc[:, a * DIM : (a + 1) * DIM].astype(BF16)

    for c in range(CHUNKS):
        part = send.at[c, pl.ds(0, N_CTX - 1)]
        pltpu.make_async_copy(part, part, send_sem.at[c]).wait()
        part = ret_send.at[c, pl.ds(0, N_CTX - 1)]
        pltpu.make_async_copy(part, part, rsend_sem.at[c]).wait()
    for i in range(2):
        pltpu.make_async_copy(halo.at[i], halo.at[i], halo_ssem.at[i]).wait()
        pltpu.make_async_copy(grad_send.at[i], grad_send.at[i], grad_ssem.at[i]).wait()
    for i, n in enumerate((N_CTX, N_CTX, N_HEAD)):
        part = cnt_recv.at[pl.ds(0, n - 1)]
        pltpu.make_async_copy(part, part, small_ssem.at[i]).wait()


def deliver(*refs):
    sources, targets, sems = refs[:10], refs[10:20], refs[20]
    copies = [pltpu.make_async_copy(s, t, sems.at[i]) for i, (s, t) in enumerate(zip(sources, targets))]
    for copy in copies:
        copy.start()
    for copy in copies:
        copy.wait()


def shards(rq, rk, rv, rg, lq, lk, lv, lg, clusters, cluster_slot, rel_bias):
    token_out = jax.ShapeDtypeStruct((TOK, DIM), BF16)
    vm = pltpu.VMEM
    dma = pltpu.SemaphoreType.DMA
    scratch = [
        vm((TOK, 4 * DIM), BF16),
        vm((TOK, DIM), BF16), vm((TOK, DIM), BF16), vm((TOK, DIM), BF16), vm((TOK, DIM), BF16),
        vm((CHUNKS, N_CTX, 4, ROWS, DIM), BF16), vm((CHUNKS, N_CTX, 4, ROWS, DIM), BF16),
        vm((CHUNKS, N_CTX, 4, ROWS, DIM), BF16), vm((CHUNKS, N_CTX, 4, ROWS, DIM), BF16),
        vm((2, WINDOW, DIM), BF16), vm((2, WINDOW, DIM), BF16), vm((2, WINDOW, DIM), BF16),
        vm((1, DIM), F32), vm((N_CTX, 1, DIM), F32),
        vm((1, DIM), F32), vm((N_CTX, 1, DIM), F32),
        vm((1, DIM), F32), vm((N_HEAD, 1, DIM), F32),
        vm((1, TOK), I32), vm((CHUNKS, TOK, SPAN), BF16), vm((CHUNKS, 1, SPAN), F32),
        vm((SPAN, SPAN), F32), vm((WINDOW, 2 * WINDOW), F32), vm((TOK, 4 * DIM), F32),
        vm((2, TOK, DIM), F32),
        vm((WINDOW, 2 * WINDOW), F32),
        dma((8,)),
        dma((CHUNKS,)), dma((CHUNKS,)), dma((CHUNKS,)), dma((CHUNKS,)),
        dma((2,)), dma((2,)), dma((2,)), dma((2,)), dma((3,)), dma((3,)), dma((3,)),
    ]
    anywhere = pl.BlockSpec(memory_space=pl.ANY)
    small = [jax.ShapeDtypeStruct((CHUNKS, 2, DIM), F32), jax.ShapeDtypeStruct((1, DIM), F32)]
    packed = pl.pallas_call(
        kernel,
        out_shape=[token_out] * 8 + small,
        in_specs=[anywhere] * 8 + [pl.BlockSpec(memory_space=pltpu.VMEM)] * 3,
        out_specs=[pl.BlockSpec(memory_space=pltpu.VMEM)] * 10,
        scratch_shapes=scratch,
        compiler_params=pltpu.CompilerParams(
            collective_id=0, has_side_effects=True, vmem_limit_bytes=VMEM_GRANT
        ),
        name="routing",
    )(rq, rk, rv, rg, lq, lk, lv, lg, clusters, cluster_slot, rel_bias.reshape(1, DIM))
    ro, rdq, rdk, rdv, lo, ldq, ldk, ldv, cent, bias = pl.pallas_call(
        deliver,
        out_shape=[token_out] * 8 + small,
        in_specs=[anywhere] * 10,
        out_specs=[anywhere] * 10,
        scratch_shapes=[dma((10,))],
        compiler_params=pltpu.CompilerParams(vmem_limit_bytes=VMEM_GRANT),
        name="deliver",
    )(*packed)
    return (
        ro, rdq, rdk, rdv, cent.reshape(1, 8, DIM), lo, ldq, ldk, ldv, bias.reshape(DIM),
    )


def solution(mesh):
    tokens = P("ctx", "head")
    return jax.shard_map(
        shards,
        mesh=mesh,
        in_specs=(tokens,) * 8 + (P("head", "ctx"), P("head", None), P()),
        out_specs=(tokens,) * 4 + (P("head", "ctx", None),) + (tokens,) * 4 + (P(),),
        check_vma=False,
    )
```

```python
import functools

import jax
import jax.numpy as jnp
from jax import lax
from jax.experimental import pallas as pl
from jax.experimental.pallas import tpu as pltpu
from jax.sharding import PartitionSpec as P

TOK = 512
DIM = 128
WINDOW = 128
N_CTX = 16
N_HEAD = 8
CHUNKS = 4
ROWS = 16
SPAN = N_CTX * ROWS
NEG = -1e30
EPSILON = 1e-06
VMEM_GRANT = 54140 * 1024
SCALE = DIM ** (-0.5)
F32 = jnp.float32
BF16 = jnp.bfloat16
I32 = jnp.int32
MESH = pl.DeviceIdType.MESH


def iota(shape, dim):
    return lax.broadcasted_iota(I32, shape, dim)


def mm(a, b):
    return jnp.dot(a, b, preferred_element_type=F32)


def mm_nt(a, b):
    return lax.dot_general(a, b, (((1,), (1,)), ((), ())), preferred_element_type=F32)


def mm_tn(a, b):
    return lax.dot_general(a, b, (((0,), (0,)), ((), ())), preferred_element_type=F32)


def landed(part, sem):
    pltpu.make_async_copy(part, part, sem).wait()


def attention(q, k, v, g, mask):
    scores = mm_nt(q, k) * SCALE + mask
    top = jnp.max(scores, axis=-1, keepdims=True)
    e = jnp.exp(scores - top)
    p = e / jnp.sum(e, axis=-1, keepdims=True)
    p_low = p.astype(BF16)
    dp = mm_nt(g, v)
    ds = p * (dp - jnp.sum(p * dp, axis=-1, keepdims=True))
    ds_low = ds.astype(BF16)
    out = mm(p_low, v)
    dq = mm(ds_low, k) * SCALE
    dk = mm_tn(ds_low, q) * SCALE
    dv = mm_tn(p_low, g)
    return out, dq, dk, dv, ds


def kernel(
    rq, rk, rv, rg, lq, lk, lv, lg, cl, slot, rb,
    o_ro, o_rdq, o_rdk, o_rdv, o_lo, o_ldq, o_ldk, o_ldv, o_cent, o_bias,
    tok, wq, wk, wv, wg,
    send, recv, ret_send, ret_recv, halo, grad_send, grad_recv,
    cnt_send, cnt_recv, bias_a, bias_a_recv, bias_b, bias_b_recv, bias_c, bias_d,
    flat_v, back_hot, live_v, mask_v, wbias, acc, wacc,
    bias_v,
    in_sem, send_sem, recv_sem, rsend_sem, rrecv_sem,
    halo_ssem, halo_rsem, grad_ssem, grad_rsem, small_ssem, small_rsem, go_sem,
):
    me = lax.axis_index("ctx")
    my_head = lax.axis_index("head")
    my_x = lax.rem(me, 4)
    my_y = lax.div(me, 4)
    ahead = lax.rem(me + 1, N_CTX)
    behind = lax.rem(me + N_CTX - 1, N_CTX)

    def peer(step):
        px = lax.rem(my_x + lax.rem(step, 4), 4)
        py = lax.rem(my_y + lax.div(step, 4), 4)
        return py * 4 + px

    lead = me == 0
    barrier = pltpu.get_barrier_semaphore()

    @pl.loop(1, N_CTX)
    def _(step):
        to = peer(step)

        @pl.when(to != 0)
        def _():
            pl.semaphore_signal(barrier, inc=1, device_id={"ctx": to}, device_id_type=MESH)

    @pl.when(lead)
    def _():
        @pl.loop(1, N_HEAD)
        def _(step):
            pl.semaphore_signal(
                barrier, inc=1, device_id={"head": lax.rem(my_head + step, N_HEAD)}, device_id_type=MESH
            )

    def fetch(src, dst, i):
        copy = pltpu.make_async_copy(src, dst, in_sem.at[i])
        copy.start()
        return copy

    routed_in = [
        fetch(src, tok.at[:, pl.ds(i * DIM, DIM)], i) for i, src in enumerate((rq, rk, rv, rg))
    ]
    local_in = [fetch(src, dst, 4 + i) for i, (src, dst) in enumerate(((lk, wk), (lv, wv), (lq, wq), (lg, wg)))]

    cluster_rows = iota((DIM, TOK), 0)
    named = (cl[...] == cluster_rows).astype(F32).astype(BF16)
    slots16 = jnp.broadcast_to(slot[...].astype(F32), (16, DIM)).astype(BF16)
    slot_of = mm(slots16, named)[0:1].astype(I32)
    in_slot = slot_of == cluster_rows
    placed = in_slot.astype(F32).astype(BF16)
    upto = (iota((TOK, TOK), 0) <= iota((TOK, TOK), 1)).astype(F32).astype(BF16)
    ranks = mm(placed, upto)
    rank = jnp.sum(jnp.where(in_slot, ranks, 0.0), axis=0, keepdims=True).astype(I32) - 1
    flat = (
        ((slot_of >> 1) & 3) * SPAN + (slot_of >> 3) * ROWS + (slot_of & 1) * 8 + rank
    )
    flat_v[...] = flat
    cnt_send[...] = mm_nt(jnp.ones((16, TOK), BF16), placed)[0:1]

    for copy in routed_in:
        copy.wait()

    def pack(c):
        hot = (flat_v[...] == iota((SPAN, TOK), 0) + c * SPAN).astype(F32).astype(BF16)
        rows = mm(hot, tok[...]).astype(BF16)
        for a in range(4):
            send[c, :, a] = rows[:, a * DIM : (a + 1) * DIM].reshape(N_CTX, ROWS, DIM)

    @pl.when(me != 0)
    def _():
        pl.semaphore_wait(barrier, N_CTX - 1)
        pl.semaphore_signal(go_sem, inc=1, device_id={"ctx": 0}, device_id_type=MESH)

    @pl.when(lead)
    def _():
        pl.semaphore_wait(go_sem, N_CTX - 1)


    for copy in local_in[:2]:
        copy.wait()
    for i, src in enumerate((wk, wv)):
        pltpu.make_async_remote_copy(
            src.at[pl.ds(TOK - WINDOW, WINDOW)], halo.at[i], halo_ssem.at[i], halo_rsem.at[i],
            device_id={"ctx": ahead}, device_id_type=MESH,
        ).start()

    @pl.loop(1, N_CTX)
    def _(step):
        pltpu.make_async_remote_copy(
            cnt_send, cnt_recv.at[me], small_ssem.at[0], small_rsem.at[0],
            device_id={"ctx": peer(step)}, device_id_type=MESH,
        ).start()

    cnt_recv[me] = cnt_send[...]

    @pl.loop(0, CHUNKS)
    def _(c):
        pack(c)

        @pl.loop(1, N_CTX)
        def _(step):
            to = peer(step)
            pltpu.make_async_remote_copy(
                send.at[c, to], recv.at[c, me], send_sem.at[c], recv_sem.at[c],
                device_id={"ctx": to}, device_id_type=MESH,
            ).start()

        recv[c, me] = send[c, me]

    back_hot[...] = jnp.zeros_like(back_hot)
    flat_col = jnp.transpose(jnp.broadcast_to(flat.astype(F32), (8, TOK)))[:, 0:1].astype(I32)

    @pl.loop(0, CHUNKS)
    def _(c):
        back_hot[c] = (flat_col == iota((TOK, SPAN), 1) + c * SPAN).astype(F32).astype(BF16)

    row_i = iota((WINDOW, 2 * WINDOW), 0)
    col_i = iota((WINDOW, 2 * WINDOW), 1)
    bias_col = jnp.sum(
        jnp.where(iota((DIM, DIM), 0) == iota((DIM, DIM), 1), rb[...], 0.0), axis=1, keepdims=True
    )
    spread = jnp.sum(jnp.where(row_i == WINDOW - col_i, bias_col, 0.0), axis=0, keepdims=True)
    spread = jnp.broadcast_to(spread, (WINDOW, 2 * WINDOW))
    for b in range(7):
        spread = jnp.where((row_i >> b) & 1 == 1, pltpu.roll(spread, 1 << b, 1), spread)
    offset = WINDOW + row_i - col_i
    wbias[...] = jnp.where((offset >= 0) & (offset < WINDOW), spread, NEG)

    for copy in local_in[2:]:
        copy.wait()

    def local_block(b, k, v, mask):
        rows = pl.ds(b * WINDOW, WINDOW)
        out, dq, dk, dv, ds = attention(wq[rows], k, v, wg[rows], mask)
        o_lo[rows] = out.astype(BF16)
        o_ldq[rows] = dq.astype(BF16)
        return dk, dv, ds

    wacc[...] = jnp.zeros_like(wacc)
    bias_v[...] = jnp.zeros_like(bias_v)

    @pl.loop(1, 4)
    def _(b):
        at = pl.multiple_of((b - 1) * WINDOW, WINDOW)
        frame = pl.ds(at, 2 * WINDOW)
        dk, dv, ds = local_block(b, wk[frame], wv[frame], wbias[...])
        wacc[0, frame] += dk
        wacc[1, frame] += dv
        bias_v[...] += ds

    for i in range(2):
        pltpu.make_async_remote_copy(
            wk.at[pl.ds(0, WINDOW)], halo.at[i], halo_ssem.at[i], halo_rsem.at[i],
            device_id={"ctx": ahead}, device_id_type=MESH,
        ).wait_recv()
    first = jnp.where((col_i < WINDOW) & (me == 0), NEG, wbias[...])
    own = pl.ds(0, WINDOW)
    dk, dv, ds = local_block(
        0,
        jnp.concatenate([halo[0], wk[own]], axis=0),
        jnp.concatenate([halo[1], wv[own]], axis=0),
        first,
    )
    for i, d in enumerate((dk, dv)):
        grad_send[i] = d[:WINDOW].astype(BF16)
        wacc[i, own] += d[WINDOW:]
        pltpu.make_async_remote_copy(
            grad_send.at[i], grad_recv.at[i], grad_ssem.at[i], grad_rsem.at[i],
            device_id={"ctx": behind}, device_id_type=MESH,
        ).start()

    total = bias_v[...] + ds
    for b in range(7):
        total = jnp.where((row_i >> b) & 1 == 1, pltpu.roll(total, 2 * WINDOW - (1 << b), 1), total)
    by_col = jnp.sum(total, axis=0, keepdims=True)
    square = (2 * WINDOW, 2 * WINDOW)
    by_row = jnp.sum(jnp.where(iota(square, 0) == iota(square, 1), by_col, 0.0), axis=1, keepdims=True)
    tall = (2 * WINDOW, WINDOW)
    bias_a[...] = jnp.sum(
        jnp.where(iota(tall, 0) == WINDOW - iota(tall, 1), by_row, 0.0), axis=0, keepdims=True
    )

    @pl.when(me != 0)
    def _():
        pltpu.make_async_remote_copy(
            bias_a, bias_a_recv.at[me], small_ssem.at[1], small_rsem.at[1],
            device_id={"ctx": 0}, device_id_type=MESH,
        ).start()

    @pl.when(lead)
    def _():
        bias_a_recv[0] = bias_a[...]

    landed(cnt_recv.at[pl.ds(0, N_CTX - 1)], small_rsem.at[0])
    counts = jnp.concatenate([cnt_recv[s] for s in range(N_CTX)], axis=0).astype(BF16)
    wide = (DIM, CHUNKS * SPAN)
    j = iota(wide, 1)
    pick = iota(wide, 0) == me * 8 + (j >> 8) * 2 + ((j >> 3) & 1)
    picked = mm(counts, pick.astype(F32).astype(BF16))
    j = iota((N_CTX, CHUNKS * SPAN), 1)
    held = jnp.sum(
        jnp.where(iota((N_CTX, CHUNKS * SPAN), 0) == ((j >> 4) & 15), picked, 0.0), axis=0, keepdims=True
    )
    live = jnp.where((iota((1, CHUNKS * SPAN), 1) & 7).astype(F32) < held, 0.0, NEG)
    for c in range(CHUNKS):
        live_v[c] = live[:, c * SPAN : (c + 1) * SPAN]
    span = (SPAN, SPAN)
    si, sj = iota(span, 0), iota(span, 1)
    mask_v[...] = jnp.where((((si ^ sj) & 8) == 0) & (sj <= si), 0.0, NEG)

    @pl.loop(0, CHUNKS)
    def _(c):
        @pl.when(lead & (c == 1))
        def _():
            landed(bias_a_recv.at[pl.ds(0, N_CTX - 1)], small_rsem.at[1])
            bias_b[...] = jnp.sum(bias_a_recv[...], axis=0)
            bias_b_recv[my_head] = bias_b[...]
            pl.semaphore_wait(barrier, N_HEAD - 1)

            @pl.loop(1, N_HEAD)
            def _(step):
                pltpu.make_async_remote_copy(
                    bias_b, bias_b_recv.at[my_head], small_ssem.at[2], small_rsem.at[2],
                    device_id={"head": lax.rem(my_head + step, N_HEAD)}, device_id_type=MESH,
                ).start()

        landed(recv.at[c, pl.ds(0, N_CTX - 1)], recv_sem.at[c])
        q, k, v, g = (recv[c, :, a].reshape(SPAN, DIM) for a in range(4))
        out, dq, dk, dv, _ = attention(q, k, v, g, mask_v[...] + live_v[c])
        for a, r in enumerate((out, dq, dk, dv)):
            ret_send[c, :, a] = r.astype(BF16).reshape(N_CTX, ROWS, DIM)

        @pl.loop(1, N_CTX)
        def _(step):
            to = peer(step)
            pltpu.make_async_remote_copy(
                ret_send.at[c, to], ret_recv.at[c, me], rsend_sem.at[c], rrecv_sem.at[c],
                device_id={"ctx": to}, device_id_type=MESH,
            ).start()

        ret_recv[c, me] = ret_send[c, me]
        pick = (((iota((16, SPAN), 1) >> 3) & 1) == iota((16, SPAN), 0)).astype(F32).astype(BF16)
        sums = mm(pick, k)[0:2]
        o_cent[c] = sums / jnp.sqrt(jnp.mean(sums * sums, axis=-1, keepdims=True) + EPSILON)

    @pl.when(lead)
    def _():
        landed(bias_b_recv.at[pl.ds(0, N_HEAD - 1)], small_rsem.at[2])
        bias_c[...] = jnp.sum(bias_b_recv[...], axis=0)

        @pl.loop(1, N_CTX)
        def _(step):
            pltpu.make_async_remote_copy(
                bias_c, bias_d, small_ssem.at[3], small_rsem.at[3],
                device_id={"ctx": peer(step)}, device_id_type=MESH,
            ).start()

    for i in range(2):
        pltpu.make_async_remote_copy(
            grad_send.at[i], grad_recv.at[i], grad_ssem.at[i], grad_rsem.at[i],
            device_id={"ctx": behind}, device_id_type=MESH,
        ).wait_recv()
        wacc[i, pl.ds(TOK - WINDOW, WINDOW)] += grad_recv[i].astype(F32)
        (o_ldk, o_ldv)[i][...] = wacc[i].astype(BF16)
    acc[...] = jnp.zeros_like(acc)

    @pl.loop(0, CHUNKS)
    def _(c):
        landed(ret_recv.at[c, pl.ds(0, N_CTX - 1)], rrecv_sem.at[c])
        rows = jnp.concatenate([ret_recv[c, :, a].reshape(SPAN, DIM) for a in range(4)], axis=1)
        acc[...] += mm(back_hot[c], rows)

    for a, dst in enumerate((o_ro, o_rdq, o_rdk, o_rdv)):
        dst[...] = acc[:, a * DIM : (a + 1) * DIM].astype(BF16)

    for c in range(CHUNKS):
        part = send.at[c, pl.ds(0, N_CTX - 1)]
        pltpu.make_async_copy(part, part, send_sem.at[c]).wait()
        part = ret_send.at[c, pl.ds(0, N_CTX - 1)]
        pltpu.make_async_copy(part, part, rsend_sem.at[c]).wait()
    for i in range(2):
        pltpu.make_async_copy(halo.at[i], halo.at[i], halo_ssem.at[i]).wait()
        pltpu.make_async_copy(grad_send.at[i], grad_send.at[i], grad_ssem.at[i]).wait()
    landed(cnt_recv.at[pl.ds(0, N_CTX - 1)], small_ssem.at[0])

    @pl.when(lead)
    def _():
        o_bias[...] = bias_c[...]
        landed(bias_b_recv.at[pl.ds(0, N_HEAD - 1)], small_ssem.at[2])
        landed(bias_a_recv.at[pl.ds(0, N_CTX - 1)], small_ssem.at[3])

    @pl.when(me != 0)
    def _():
        landed(bias_d, small_rsem.at[3])
        o_bias[...] = bias_d[...]
        landed(bias_a, small_ssem.at[1])


def deliver(*refs):
    sources, targets, sems = refs[:10], refs[10:20], refs[20]
    copies = [pltpu.make_async_copy(s, t, sems.at[i]) for i, (s, t) in enumerate(zip(sources, targets))]
    for copy in copies:
        copy.start()
    for copy in copies:
        copy.wait()


def shards(rq, rk, rv, rg, lq, lk, lv, lg, clusters, cluster_slot, rel_bias):
    token_out = jax.ShapeDtypeStruct((TOK, DIM), BF16)
    vm = pltpu.VMEM
    dma = pltpu.SemaphoreType.DMA
    scratch = [
        vm((TOK, 4 * DIM), BF16),
        vm((TOK, DIM), BF16), vm((TOK, DIM), BF16), vm((TOK, DIM), BF16), vm((TOK, DIM), BF16),
        vm((CHUNKS, N_CTX, 4, ROWS, DIM), BF16), vm((CHUNKS, N_CTX, 4, ROWS, DIM), BF16),
        vm((CHUNKS, N_CTX, 4, ROWS, DIM), BF16), vm((CHUNKS, N_CTX, 4, ROWS, DIM), BF16),
        vm((2, WINDOW, DIM), BF16), vm((2, WINDOW, DIM), BF16), vm((2, WINDOW, DIM), BF16),
        vm((1, DIM), F32), vm((N_CTX, 1, DIM), F32),
        vm((1, DIM), F32), vm((N_CTX, 1, DIM), F32),
        vm((1, DIM), F32), vm((N_HEAD, 1, DIM), F32), vm((1, DIM), F32), vm((1, DIM), F32),
        vm((1, TOK), I32), vm((CHUNKS, TOK, SPAN), BF16), vm((CHUNKS, 1, SPAN), F32),
        vm((SPAN, SPAN), F32), vm((WINDOW, 2 * WINDOW), F32), vm((TOK, 4 * DIM), F32),
        vm((2, TOK, DIM), F32),
        vm((WINDOW, 2 * WINDOW), F32),
        dma((8,)),
        dma((CHUNKS,)), dma((CHUNKS,)), dma((CHUNKS,)), dma((CHUNKS,)),
        dma((2,)), dma((2,)), dma((2,)), dma((2,)), dma((4,)), dma((4,)), pltpu.SemaphoreType.REGULAR,
    ]
    anywhere = pl.BlockSpec(memory_space=pl.ANY)
    small = [jax.ShapeDtypeStruct((CHUNKS, 2, DIM), F32), jax.ShapeDtypeStruct((1, DIM), F32)]
    packed = pl.pallas_call(
        kernel,
        out_shape=[token_out] * 8 + small,
        in_specs=[anywhere] * 8 + [pl.BlockSpec(memory_space=pltpu.VMEM)] * 3,
        out_specs=[pl.BlockSpec(memory_space=pltpu.VMEM)] * 10,
        scratch_shapes=scratch,
        compiler_params=pltpu.CompilerParams(
            collective_id=0, has_side_effects=True, vmem_limit_bytes=VMEM_GRANT
        ),
        name="routing",
    )(rq, rk, rv, rg, lq, lk, lv, lg, clusters, cluster_slot, rel_bias.reshape(1, DIM))
    ro, rdq, rdk, rdv, lo, ldq, ldk, ldv, cent, bias = pl.pallas_call(
        deliver,
        out_shape=[token_out] * 8 + small,
        in_specs=[anywhere] * 10,
        out_specs=[anywhere] * 10,
        scratch_shapes=[dma((10,))],
        compiler_params=pltpu.CompilerParams(vmem_limit_bytes=VMEM_GRANT),
        name="deliver",
    )(*packed)
    return (
        ro, rdq, rdk, rdv, cent.reshape(1, 8, DIM), lo, ldq, ldk, ldv, bias.reshape(DIM),
    )


def solution(mesh):
    tokens = P("ctx", "head")
    return jax.shard_map(
        shards,
        mesh=mesh,
        in_specs=(tokens,) * 8 + (P("head", "ctx"), P("head", None), P()),
        out_specs=(tokens,) * 4 + (P("head", "ctx", None),) + (tokens,) * 4 + (P(),),
        check_vma=False,
    )
```

```python
import functools

import jax
import jax.numpy as jnp
from jax import lax
from jax.experimental import pallas as pl
from jax.experimental.pallas import tpu as pltpu
from jax.sharding import PartitionSpec as P

TOK = 512
DIM = 128
WINDOW = 128
N_CTX = 16
N_HEAD = 8
CHUNKS = 4
ROWS = 16
SPAN = N_CTX * ROWS
NEG = -1e30
EPSILON = 1e-06
VMEM_GRANT = 54140 * 1024
SCALE = DIM ** (-0.5)
F32 = jnp.float32
BF16 = jnp.bfloat16
I32 = jnp.int32
MESH = pl.DeviceIdType.MESH


def iota(shape, dim):
    return lax.broadcasted_iota(I32, shape, dim)


def mm(a, b):
    return jnp.dot(a, b, preferred_element_type=F32)


def mm_nt(a, b):
    return lax.dot_general(a, b, (((1,), (1,)), ((), ())), preferred_element_type=F32)


def mm_tn(a, b):
    return lax.dot_general(a, b, (((0,), (0,)), ((), ())), preferred_element_type=F32)


def landed(part, sem):
    pltpu.make_async_copy(part, part, sem).wait()


def attention(q, k, v, g, mask):
    scores = mm_nt(q, k) * SCALE + mask
    top = jnp.max(scores, axis=-1, keepdims=True)
    e = jnp.exp(scores - top)
    p = e / jnp.sum(e, axis=-1, keepdims=True)
    p_low = p.astype(BF16)
    dp = mm_nt(g, v)
    ds = p * (dp - jnp.sum(p * dp, axis=-1, keepdims=True))
    ds_low = ds.astype(BF16)
    out = mm(p_low, v)
    dq = mm(ds_low, k) * SCALE
    dk = mm_tn(ds_low, q) * SCALE
    dv = mm_tn(p_low, g)
    return out, dq, dk, dv, ds


def kernel(
    rq, rk, rv, rg, lq, lk, lv, lg, cl, slot, rb,
    o_ro, o_rdq, o_rdk, o_rdv, o_lo, o_ldq, o_ldk, o_ldv, o_cent, o_bias,
    tok, wq, wk, wv, wg,
    send, recv, ret_send, ret_recv, halo, grad_send, grad_recv,
    cnt_send, cnt_recv, bias_a, bias_a_recv, bias_b, bias_b_recv, bias_c, bias_d,
    flat_v, back_hot, live_v, mask_v, wbias, acc, wacc,
    bias_v,
    in_sem, send_sem, recv_sem, rsend_sem, rrecv_sem,
    halo_ssem, halo_rsem, grad_ssem, grad_rsem, small_ssem, small_rsem, go_sem,
):
    me = lax.axis_index("ctx")
    my_head = lax.axis_index("head")
    my_x = lax.rem(me, 4)
    my_y = lax.div(me, 4)
    ahead = lax.rem(me + 1, N_CTX)
    behind = lax.rem(me + N_CTX - 1, N_CTX)

    def peer(step):
        px = lax.rem(my_x + lax.rem(step, 4), 4)
        py = lax.rem(my_y + lax.div(step, 4), 4)
        return py * 4 + px

    lead = me == 0
    barrier = pltpu.get_barrier_semaphore()

    @pl.loop(0, N_CTX - 1)
    def _(i):
        to = peer(lax.rem(i + 9, N_CTX - 1) + 1)

        @pl.when(to != 0)
        def _():
            pl.semaphore_signal(barrier, inc=1, device_id={"ctx": to}, device_id_type=MESH)

    @pl.when(lead)
    def _():
        @pl.loop(1, N_HEAD)
        def _(step):
            pl.semaphore_signal(
                barrier, inc=1, device_id={"head": lax.rem(my_head + step, N_HEAD)}, device_id_type=MESH
            )

    def fetch(src, dst, i):
        copy = pltpu.make_async_copy(src, dst, in_sem.at[i])
        copy.start()
        return copy

    routed_in = [
        fetch(src, tok.at[:, pl.ds(i * DIM, DIM)], i) for i, src in enumerate((rq, rk, rv, rg))
    ]
    local_in = [fetch(src, dst, 4 + i) for i, (src, dst) in enumerate(((lk, wk), (lv, wv), (lq, wq), (lg, wg)))]

    cluster_rows = iota((DIM, TOK), 0)
    named = (jnp.concatenate([cl[i] for i in range(4)], axis=1) == cluster_rows).astype(F32).astype(BF16)
    slots16 = jnp.broadcast_to(slot[0].astype(F32), (16, DIM)).astype(BF16)
    slot_of = mm(slots16, named)[0:1].astype(I32)
    in_slot = slot_of == cluster_rows
    placed = in_slot.astype(F32).astype(BF16)
    upto = (iota((TOK, TOK), 0) <= iota((TOK, TOK), 1)).astype(F32).astype(BF16)
    ranks = mm(placed, upto)
    rank = jnp.sum(jnp.where(in_slot, ranks, 0.0), axis=0, keepdims=True).astype(I32) - 1
    flat = (
        ((slot_of >> 1) & 3) * SPAN + (slot_of >> 3) * ROWS + (slot_of & 1) * 8 + rank
    )
    flat_v[...] = flat
    cnt_send[...] = mm_nt(jnp.ones((16, TOK), BF16), placed)[0:1]

    for copy in routed_in:
        copy.wait()

    def pack(c):
        hot = (flat_v[...] == iota((SPAN, TOK), 0) + c * SPAN).astype(F32).astype(BF16)
        rows = mm(hot, tok[...]).astype(BF16)
        for a in range(4):
            send[c, :, a] = rows[:, a * DIM : (a + 1) * DIM].reshape(N_CTX, ROWS, DIM)

    pack(0)

    @pl.when(me != 0)
    def _():
        pl.semaphore_wait(barrier, N_CTX - 1)
        pl.semaphore_signal(go_sem, inc=1, device_id={"ctx": 0}, device_id_type=MESH)

    @pl.when(lead)
    def _():
        pl.semaphore_wait(go_sem, N_CTX - 1)


    for copy in local_in[:2]:
        copy.wait()
    for i, src in enumerate((wk, wv)):
        pltpu.make_async_remote_copy(
            src.at[pl.ds(TOK - WINDOW, WINDOW)], halo.at[i], halo_ssem.at[i], halo_rsem.at[i],
            device_id={"ctx": ahead}, device_id_type=MESH,
        ).start()

    cnt_recv[me] = cnt_send[...]

    @pl.loop(0, CHUNKS)
    def _(c):
        @pl.loop(1, N_CTX)
        def _(step):
            to = peer(step)
            pltpu.make_async_remote_copy(
                send.at[c, to], recv.at[c, me], send_sem.at[c], recv_sem.at[c],
                device_id={"ctx": to}, device_id_type=MESH,
            ).start()

        @pl.when(c == 0)
        def _():
            @pl.loop(1, N_CTX)
            def _(step):
                pltpu.make_async_remote_copy(
                    cnt_send, cnt_recv.at[me], small_ssem.at[0], small_rsem.at[0],
                    device_id={"ctx": peer(step)}, device_id_type=MESH,
                ).start()

        recv[c, me] = send[c, me]

        @pl.when(c < CHUNKS - 1)
        def _():
            pack(c + 1)

    back_hot[...] = jnp.zeros_like(back_hot)
    flat_col = jnp.transpose(jnp.broadcast_to(flat.astype(F32), (8, TOK)))[:, 0:1].astype(I32)

    @pl.loop(0, CHUNKS)
    def _(c):
        back_hot[c] = (flat_col == iota((TOK, SPAN), 1) + c * SPAN).astype(F32).astype(BF16)

    row_i = iota((WINDOW, 2 * WINDOW), 0)
    col_i = iota((WINDOW, 2 * WINDOW), 1)
    bias_col = jnp.sum(
        jnp.where(iota((DIM, DIM), 0) == iota((DIM, DIM), 1), rb[...], 0.0), axis=1, keepdims=True
    )
    spread = jnp.sum(jnp.where(row_i == WINDOW - col_i, bias_col, 0.0), axis=0, keepdims=True)
    spread = jnp.broadcast_to(spread, (WINDOW, 2 * WINDOW))
    for b in range(7):
        spread = jnp.where((row_i >> b) & 1 == 1, pltpu.roll(spread, 1 << b, 1), spread)
    offset = WINDOW + row_i - col_i
    wbias[...] = jnp.where((offset >= 0) & (offset < WINDOW), spread, NEG)

    for copy in local_in[2:]:
        copy.wait()

    def local_block(b, k, v, mask):
        rows = pl.ds(b * WINDOW, WINDOW)
        out, dq, dk, dv, ds = attention(wq[rows], k, v, wg[rows], mask)
        o_lo[rows] = out.astype(BF16)
        o_ldq[rows] = dq.astype(BF16)
        return dk, dv, ds

    wacc[...] = jnp.zeros_like(wacc)
    bias_v[...] = jnp.zeros_like(bias_v)

    @pl.loop(1, 4)
    def _(b):
        at = pl.multiple_of((b - 1) * WINDOW, WINDOW)
        frame = pl.ds(at, 2 * WINDOW)
        dk, dv, ds = local_block(b, wk[frame], wv[frame], wbias[...])
        wacc[0, frame] += dk
        wacc[1, frame] += dv
        bias_v[...] += ds

    for i in range(2):
        pltpu.make_async_remote_copy(
            wk.at[pl.ds(0, WINDOW)], halo.at[i], halo_ssem.at[i], halo_rsem.at[i],
            device_id={"ctx": ahead}, device_id_type=MESH,
        ).wait_recv()
    first = jnp.where((col_i < WINDOW) & (me == 0), NEG, wbias[...])
    own = pl.ds(0, WINDOW)
    dk, dv, ds = local_block(
        0,
        jnp.concatenate([halo[0], wk[own]], axis=0),
        jnp.concatenate([halo[1], wv[own]], axis=0),
        first,
    )
    for i, d in enumerate((dk, dv)):
        grad_send[i] = d[:WINDOW].astype(BF16)
        wacc[i, own] += d[WINDOW:]
        pltpu.make_async_remote_copy(
            grad_send.at[i], grad_recv.at[i], grad_ssem.at[i], grad_rsem.at[i],
            device_id={"ctx": behind}, device_id_type=MESH,
        ).start()

    total = bias_v[...] + ds
    for b in range(7):
        total = jnp.where((row_i >> b) & 1 == 1, pltpu.roll(total, 2 * WINDOW - (1 << b), 1), total)
    by_col = jnp.sum(total, axis=0, keepdims=True)
    square = (2 * WINDOW, 2 * WINDOW)
    by_row = jnp.sum(jnp.where(iota(square, 0) == iota(square, 1), by_col, 0.0), axis=1, keepdims=True)
    tall = (2 * WINDOW, WINDOW)
    bias_a[...] = jnp.sum(
        jnp.where(iota(tall, 0) == WINDOW - iota(tall, 1), by_row, 0.0), axis=0, keepdims=True
    )

    @pl.when(me != 0)
    def _():
        pltpu.make_async_remote_copy(
            bias_a, bias_a_recv.at[me], small_ssem.at[1], small_rsem.at[1],
            device_id={"ctx": 0}, device_id_type=MESH,
        ).start()

    @pl.when(lead)
    def _():
        bias_a_recv[0] = bias_a[...]

    landed(cnt_recv.at[pl.ds(0, N_CTX - 1)], small_rsem.at[0])
    counts = jnp.concatenate([cnt_recv[s] for s in range(N_CTX)], axis=0).astype(BF16)
    wide = (DIM, CHUNKS * SPAN)
    j = iota(wide, 1)
    pick = iota(wide, 0) == me * 8 + (j >> 8) * 2 + ((j >> 3) & 1)
    picked = mm(counts, pick.astype(F32).astype(BF16))
    j = iota((N_CTX, CHUNKS * SPAN), 1)
    held = jnp.sum(
        jnp.where(iota((N_CTX, CHUNKS * SPAN), 0) == ((j >> 4) & 15), picked, 0.0), axis=0, keepdims=True
    )
    live = jnp.where((iota((1, CHUNKS * SPAN), 1) & 7).astype(F32) < held, 0.0, NEG)
    for c in range(CHUNKS):
        live_v[c] = live[:, c * SPAN : (c + 1) * SPAN]
    span = (SPAN, SPAN)
    si, sj = iota(span, 0), iota(span, 1)
    mask_v[...] = jnp.where((((si ^ sj) & 8) == 0) & (sj <= si), 0.0, NEG)

    @pl.loop(0, CHUNKS)
    def _(c):
        @pl.when(lead & (c == 1))
        def _():
            landed(bias_a_recv.at[pl.ds(0, N_CTX - 1)], small_rsem.at[1])
            bias_b[...] = jnp.sum(bias_a_recv[...], axis=0)
            bias_b_recv[my_head] = bias_b[...]
            pl.semaphore_wait(barrier, N_HEAD - 1)

            @pl.loop(1, N_HEAD)
            def _(step):
                pltpu.make_async_remote_copy(
                    bias_b, bias_b_recv.at[my_head], small_ssem.at[2], small_rsem.at[2],
                    device_id={"head": lax.rem(my_head + step, N_HEAD)}, device_id_type=MESH,
                ).start()

        landed(recv.at[c, pl.ds(0, N_CTX - 1)], recv_sem.at[c])
        q, k, v, g = (recv[c, :, a].reshape(SPAN, DIM) for a in range(4))
        out, dq, dk, dv, _ = attention(q, k, v, g, mask_v[...] + live_v[c])
        for a, r in enumerate((out, dq, dk, dv)):
            ret_send[c, :, a] = r.astype(BF16).reshape(N_CTX, ROWS, DIM)

        @pl.loop(1, N_CTX)
        def _(step):
            to = peer(step)
            pltpu.make_async_remote_copy(
                ret_send.at[c, to], ret_recv.at[c, me], rsend_sem.at[c], rrecv_sem.at[c],
                device_id={"ctx": to}, device_id_type=MESH,
            ).start()

        ret_recv[c, me] = ret_send[c, me]
        pick = (((iota((16, SPAN), 1) >> 3) & 1) == iota((16, SPAN), 0)).astype(F32).astype(BF16)
        sums = mm(pick, k)[0:2]
        o_cent[c] = sums / jnp.sqrt(jnp.mean(sums * sums, axis=-1, keepdims=True) + EPSILON)

    @pl.when(lead)
    def _():
        landed(bias_b_recv.at[pl.ds(0, N_HEAD - 1)], small_rsem.at[2])
        bias_c[...] = jnp.sum(bias_b_recv[...], axis=0)

        @pl.loop(1, N_CTX)
        def _(step):
            pltpu.make_async_remote_copy(
                bias_c, bias_d, small_ssem.at[3], small_rsem.at[3],
                device_id={"ctx": peer(step)}, device_id_type=MESH,
            ).start()

    for i in range(2):
        pltpu.make_async_remote_copy(
            grad_send.at[i], grad_recv.at[i], grad_ssem.at[i], grad_rsem.at[i],
            device_id={"ctx": behind}, device_id_type=MESH,
        ).wait_recv()
        wacc[i, pl.ds(TOK - WINDOW, WINDOW)] += grad_recv[i].astype(F32)
        (o_ldk, o_ldv)[i][...] = wacc[i].astype(BF16)
    acc[...] = jnp.zeros_like(acc)

    @pl.loop(0, CHUNKS)
    def _(c):
        landed(ret_recv.at[c, pl.ds(0, N_CTX - 1)], rrecv_sem.at[c])
        rows = jnp.concatenate([ret_recv[c, :, a].reshape(SPAN, DIM) for a in range(4)], axis=1)
        acc[...] += mm(back_hot[c], rows)

    for a, dst in enumerate((o_ro, o_rdq, o_rdk, o_rdv)):
        dst[...] = acc[:, a * DIM : (a + 1) * DIM].astype(BF16)

    for c in range(CHUNKS):
        part = send.at[c, pl.ds(0, N_CTX - 1)]
        pltpu.make_async_copy(part, part, send_sem.at[c]).wait()
        part = ret_send.at[c, pl.ds(0, N_CTX - 1)]
        pltpu.make_async_copy(part, part, rsend_sem.at[c]).wait()
    for i in range(2):
        pltpu.make_async_copy(halo.at[i], halo.at[i], halo_ssem.at[i]).wait()
        pltpu.make_async_copy(grad_send.at[i], grad_send.at[i], grad_ssem.at[i]).wait()
    landed(cnt_recv.at[pl.ds(0, N_CTX - 1)], small_ssem.at[0])

    @pl.when(lead)
    def _():
        o_bias[...] = bias_c[...]
        landed(bias_b_recv.at[pl.ds(0, N_HEAD - 1)], small_ssem.at[2])
        landed(bias_a_recv.at[pl.ds(0, N_CTX - 1)], small_ssem.at[3])

    @pl.when(me != 0)
    def _():
        landed(bias_d, small_rsem.at[3])
        o_bias[...] = bias_d[...]
        landed(bias_a, small_ssem.at[1])


def deliver(*refs):
    sources, targets, sems = refs[:10], refs[10:20], refs[20]
    copies = [pltpu.make_async_copy(s, t, sems.at[i]) for i, (s, t) in enumerate(zip(sources, targets))]
    for copy in copies:
        copy.start()
    for copy in copies:
        copy.wait()


def shards(rq, rk, rv, rg, lq, lk, lv, lg, clusters, cluster_slot, rel_bias):
    token_out = jax.ShapeDtypeStruct((TOK, DIM), BF16)
    vm = pltpu.VMEM
    dma = pltpu.SemaphoreType.DMA
    scratch = [
        vm((TOK, 4 * DIM), BF16),
        vm((TOK, DIM), BF16), vm((TOK, DIM), BF16), vm((TOK, DIM), BF16), vm((TOK, DIM), BF16),
        vm((CHUNKS, N_CTX, 4, ROWS, DIM), BF16), vm((CHUNKS, N_CTX, 4, ROWS, DIM), BF16),
        vm((CHUNKS, N_CTX, 4, ROWS, DIM), BF16), vm((CHUNKS, N_CTX, 4, ROWS, DIM), BF16),
        vm((2, WINDOW, DIM), BF16), vm((2, WINDOW, DIM), BF16), vm((2, WINDOW, DIM), BF16),
        vm((1, DIM), F32), vm((N_CTX, 1, DIM), F32),
        vm((1, DIM), F32), vm((N_CTX, 1, DIM), F32),
        vm((1, DIM), F32), vm((N_HEAD, 1, DIM), F32), vm((1, DIM), F32), vm((1, DIM), F32),
        vm((1, TOK), I32), vm((CHUNKS, TOK, SPAN), BF16), vm((CHUNKS, 1, SPAN), F32),
        vm((SPAN, SPAN), F32), vm((WINDOW, 2 * WINDOW), F32), vm((TOK, 4 * DIM), F32),
        vm((2, TOK, DIM), F32),
        vm((WINDOW, 2 * WINDOW), F32),
        dma((8,)),
        dma((CHUNKS,)), dma((CHUNKS,)), dma((CHUNKS,)), dma((CHUNKS,)),
        dma((2,)), dma((2,)), dma((2,)), dma((2,)), dma((4,)), dma((4,)), pltpu.SemaphoreType.REGULAR,
    ]
    anywhere = pl.BlockSpec(memory_space=pl.ANY)
    small = [jax.ShapeDtypeStruct((CHUNKS, 2, DIM), F32), jax.ShapeDtypeStruct((1, DIM), F32)]
    packed = pl.pallas_call(
        kernel,
        out_shape=[token_out] * 8 + small,
        in_specs=[anywhere] * 8 + [pl.BlockSpec(memory_space=pltpu.VMEM)] * 3,
        out_specs=[pl.BlockSpec(memory_space=pltpu.VMEM)] * 10,
        scratch_shapes=scratch,
        compiler_params=pltpu.CompilerParams(
            collective_id=0, has_side_effects=True, vmem_limit_bytes=VMEM_GRANT
        ),
        name="routing",
    )(rq, rk, rv, rg, lq, lk, lv, lg, clusters.reshape(4, 1, DIM), cluster_slot.reshape(1, 1, DIM), rel_bias.reshape(1, DIM))
    ro, rdq, rdk, rdv, lo, ldq, ldk, ldv, cent, bias = pl.pallas_call(
        deliver,
        out_shape=[token_out] * 8 + small,
        in_specs=[anywhere] * 10,
        out_specs=[anywhere] * 10,
        scratch_shapes=[dma((10,))],
        compiler_params=pltpu.CompilerParams(vmem_limit_bytes=VMEM_GRANT),
        name="deliver",
    )(*packed)
    return (
        ro, rdq, rdk, rdv, cent.reshape(1, 8, DIM), lo, ldq, ldk, ldv, bias.reshape(DIM),
    )


def solution(mesh):
    tokens = P("ctx", "head")
    return jax.shard_map(
        shards,
        mesh=mesh,
        in_specs=(tokens,) * 8 + (P("head", "ctx"), P("head", None), P()),
        out_specs=(tokens,) * 4 + (P("head", "ctx", None),) + (tokens,) * 4 + (P(),),
        check_vma=False,
    )
```

```python
import functools

import jax
import jax.numpy as jnp
from jax import lax
from jax.experimental import pallas as pl
from jax.experimental.pallas import tpu as pltpu
from jax.sharding import PartitionSpec as P

TOK = 512
DIM = 128
WINDOW = 128
N_CTX = 16
N_HEAD = 8
CHUNKS = 4
ROWS = 16
SPAN = N_CTX * ROWS
NEG = -1e30
EPSILON = 1e-06
VMEM_GRANT = 54140 * 1024
SCALE = DIM ** (-0.5)
F32 = jnp.float32
BF16 = jnp.bfloat16
I32 = jnp.int32
MESH = pl.DeviceIdType.MESH


def iota(shape, dim):
    return lax.broadcasted_iota(I32, shape, dim)


def mm(a, b):
    return jnp.dot(a, b, preferred_element_type=F32)


def mm_nt(a, b):
    return lax.dot_general(a, b, (((1,), (1,)), ((), ())), preferred_element_type=F32)


def mm_tn(a, b):
    return lax.dot_general(a, b, (((0,), (0,)), ((), ())), preferred_element_type=F32)


def landed(part, sem):
    pltpu.make_async_copy(part, part, sem).wait()


def attention(q, k, v, g, mask):
    scores = mm_nt(q, k) * SCALE + mask
    top = jnp.max(scores, axis=-1, keepdims=True)
    e = jnp.exp(scores - top)
    p = e / jnp.sum(e, axis=-1, keepdims=True)
    p_low = p.astype(BF16)
    dp = mm_nt(g, v)
    ds = p * (dp - jnp.sum(p * dp, axis=-1, keepdims=True))
    ds_low = ds.astype(BF16)
    out = mm(p_low, v)
    dq = mm(ds_low, k) * SCALE
    dk = mm_tn(ds_low, q) * SCALE
    dv = mm_tn(p_low, g)
    return out, dq, dk, dv, ds


def kernel(
    rq, rk, rv, rg, lq, lk, lv, lg, cl, slot, rb,
    o_ro, o_rdq, o_rdk, o_rdv, o_lo, o_ldq, o_ldk, o_ldv, o_cent, o_bias,
    tok, wq, wk, wv, wg,
    send, recv, ret_send, ret_recv, halo, grad_send, grad_recv,
    cnt_send, cnt_recv, bias_a, bias_a_recv, bias_b, bias_b_recv, bias_c, bias_d,
    flat_v, back_hot, live_v, mask_v, wbias, acc, wacc,
    bias_v,
    in_sem, send_sem, recv_sem, rsend_sem, rrecv_sem,
    halo_ssem, halo_rsem, grad_ssem, grad_rsem, small_ssem, small_rsem, go_sem,
):
    me = lax.axis_index("ctx")
    my_head = lax.axis_index("head")
    my_x = lax.rem(me, 4)
    my_y = lax.div(me, 4)
    ahead = lax.rem(me + 1, N_CTX)
    behind = lax.rem(me + N_CTX - 1, N_CTX)

    def peer(step):
        low, high = lax.rem(step, 4), lax.div(step, 4)
        odd = lax.rem(my_head, 2)
        px = lax.rem(my_x + low + odd * (high - low), 4)
        py = lax.rem(my_y + high + odd * (low - high), 4)
        return py * 4 + px

    lead = me == 0
    barrier = pltpu.get_barrier_semaphore()

    @pl.loop(0, N_CTX - 1)
    def _(i):
        to = peer(lax.rem(i + 9, N_CTX - 1) + 1)

        @pl.when(to != 0)
        def _():
            pl.semaphore_signal(barrier, inc=1, device_id={"ctx": to}, device_id_type=MESH)

    @pl.when(lead)
    def _():
        @pl.loop(1, N_HEAD)
        def _(step):
            pl.semaphore_signal(
                barrier, inc=1, device_id={"head": lax.rem(my_head + step, N_HEAD)}, device_id_type=MESH
            )

    def fetch(src, dst, i):
        copy = pltpu.make_async_copy(src, dst, in_sem.at[i])
        copy.start()
        return copy

    routed_in = [
        fetch(src, tok.at[:, pl.ds(i * DIM, DIM)], i) for i, src in enumerate((rq, rk, rv, rg))
    ]
    local_in = [fetch(src, dst, 4 + i) for i, (src, dst) in enumerate(((lk, wk), (lv, wv), (lq, wq), (lg, wg)))]

    cluster_rows = iota((DIM, TOK), 0)
    named = (jnp.concatenate([cl[i] for i in range(4)], axis=1) == cluster_rows).astype(F32).astype(BF16)
    slots16 = jnp.broadcast_to(slot[0].astype(F32), (16, DIM)).astype(BF16)
    slot_of = mm(slots16, named)[0:1].astype(I32)
    in_slot = slot_of == cluster_rows
    placed = in_slot.astype(F32).astype(BF16)
    upto = (iota((TOK, TOK), 0) <= iota((TOK, TOK), 1)).astype(F32).astype(BF16)
    ranks = mm(placed, upto)
    rank = jnp.sum(jnp.where(in_slot, ranks, 0.0), axis=0, keepdims=True).astype(I32) - 1
    flat = (
        ((slot_of >> 1) & 3) * SPAN + (slot_of >> 3) * ROWS + (slot_of & 1) * 8 + rank
    )
    flat_v[...] = flat
    cnt_send[...] = mm_nt(jnp.ones((16, TOK), BF16), placed)[0:1]

    for copy in routed_in:
        copy.wait()

    def pack(c):
        hot = (flat_v[...] == iota((SPAN, TOK), 0) + c * SPAN).astype(F32).astype(BF16)
        rows = mm(hot, tok[...]).astype(BF16)
        for a in range(4):
            send[c, :, a] = rows[:, a * DIM : (a + 1) * DIM].reshape(N_CTX, ROWS, DIM)

    pack(0)

    @pl.when(me != 0)
    def _():
        pl.semaphore_wait(barrier, N_CTX - 1)
        pl.semaphore_signal(go_sem, inc=1, device_id={"ctx": 0}, device_id_type=MESH)

    @pl.when(lead)
    def _():
        pl.semaphore_wait(go_sem, N_CTX - 1)


    for copy in local_in[:2]:
        copy.wait()
    cnt_recv[me] = cnt_send[...]

    @pl.loop(0, CHUNKS)
    def _(c):
        @pl.loop(1, N_CTX)
        def _(step):
            to = peer(step)
            pltpu.make_async_remote_copy(
                send.at[c, to], recv.at[c, me], send_sem.at[c], recv_sem.at[c],
                device_id={"ctx": to}, device_id_type=MESH,
            ).start()

            @pl.when((c == 0) & (step <= WINDOW // ROWS))
            def _():
                piece = pl.ds(pl.multiple_of((step - 1) * ROWS, ROWS), ROWS)
                tail = pl.ds(pl.multiple_of(TOK - WINDOW + (step - 1) * ROWS, ROWS), ROWS)
                for i, src in enumerate((wk, wv)):
                    pltpu.make_async_remote_copy(
                        src.at[tail], halo.at[i, piece], halo_ssem.at[i], halo_rsem.at[i],
                        device_id={"ctx": ahead}, device_id_type=MESH,
                    ).start()

        @pl.when(c == 0)
        def _():
            @pl.loop(1, N_CTX)
            def _(step):
                pltpu.make_async_remote_copy(
                    cnt_send, cnt_recv.at[me], small_ssem.at[0], small_rsem.at[0],
                    device_id={"ctx": peer(step)}, device_id_type=MESH,
                ).start()

        recv[c, me] = send[c, me]

        @pl.when(c < CHUNKS - 1)
        def _():
            pack(c + 1)

    flat_col = jnp.transpose(jnp.broadcast_to(flat.astype(F32), (8, TOK)))[:, 0:1].astype(I32)

    @pl.loop(0, CHUNKS)
    def _(c):
        back_hot[c] = (flat_col == iota((TOK, SPAN), 1) + c * SPAN).astype(F32).astype(BF16)

    row_i = iota((WINDOW, 2 * WINDOW), 0)
    col_i = iota((WINDOW, 2 * WINDOW), 1)
    bias_col = jnp.sum(
        jnp.where(iota((DIM, DIM), 0) == iota((DIM, DIM), 1), rb[...], 0.0), axis=1, keepdims=True
    )
    spread = jnp.sum(jnp.where(row_i == WINDOW - col_i, bias_col, 0.0), axis=0, keepdims=True)
    spread = jnp.broadcast_to(spread, (WINDOW, 2 * WINDOW))
    for b in range(7):
        spread = jnp.where((row_i >> b) & 1 == 1, pltpu.roll(spread, 1 << b, 1), spread)
    offset = WINDOW + row_i - col_i
    wbias[...] = jnp.where((offset >= 0) & (offset < WINDOW), spread, NEG)

    for copy in local_in[2:]:
        copy.wait()

    def local_block(b, k, v, mask):
        rows = pl.ds(b * WINDOW, WINDOW)
        out, dq, dk, dv, ds = attention(wq[rows], k, v, wg[rows], mask)
        o_lo[rows] = out.astype(BF16)
        o_ldq[rows] = dq.astype(BF16)
        return dk, dv, ds

    wacc[...] = jnp.zeros_like(wacc)
    bias_v[...] = jnp.zeros_like(bias_v)

    @pl.loop(1, 4)
    def _(b):
        at = pl.multiple_of((b - 1) * WINDOW, WINDOW)
        frame = pl.ds(at, 2 * WINDOW)
        dk, dv, ds = local_block(b, wk[frame], wv[frame], wbias[...])
        wacc[0, frame] += dk
        wacc[1, frame] += dv
        bias_v[...] += ds

    for i in range(2):
        pltpu.make_async_remote_copy(
            wk.at[pl.ds(0, WINDOW)], halo.at[i], halo_ssem.at[i], halo_rsem.at[i],
            device_id={"ctx": ahead}, device_id_type=MESH,
        ).wait_recv()
    first = jnp.where((col_i < WINDOW) & (me == 0), NEG, wbias[...])
    own = pl.ds(0, WINDOW)
    dk, dv, ds = local_block(
        0,
        jnp.concatenate([halo[0], wk[own]], axis=0),
        jnp.concatenate([halo[1], wv[own]], axis=0),
        first,
    )
    for i, d in enumerate((dk, dv)):
        grad_send[i] = d[:WINDOW].astype(BF16)
        wacc[i, own] += d[WINDOW:]
        pltpu.make_async_remote_copy(
            grad_send.at[i], grad_recv.at[i], grad_ssem.at[i], grad_rsem.at[i],
            device_id={"ctx": behind}, device_id_type=MESH,
        ).start()

    total = bias_v[...] + ds
    for b in range(7):
        total = jnp.where((row_i >> b) & 1 == 1, pltpu.roll(total, 2 * WINDOW - (1 << b), 1), total)
    by_col = jnp.sum(total, axis=0, keepdims=True)
    square = (2 * WINDOW, 2 * WINDOW)
    by_row = jnp.sum(jnp.where(iota(square, 0) == iota(square, 1), by_col, 0.0), axis=1, keepdims=True)
    tall = (2 * WINDOW, WINDOW)
    bias_a[...] = jnp.sum(
        jnp.where(iota(tall, 0) == WINDOW - iota(tall, 1), by_row, 0.0), axis=0, keepdims=True
    )

    @pl.when(me != 0)
    def _():
        pltpu.make_async_remote_copy(
            bias_a, bias_a_recv.at[me], small_ssem.at[1], small_rsem.at[1],
            device_id={"ctx": 0}, device_id_type=MESH,
        ).start()

    @pl.when(lead)
    def _():
        bias_a_recv[0] = bias_a[...]

    landed(cnt_recv.at[pl.ds(0, N_CTX - 1)], small_rsem.at[0])
    counts = jnp.concatenate([cnt_recv[s] for s in range(N_CTX)], axis=0).astype(BF16)
    wide = (DIM, CHUNKS * SPAN)
    j = iota(wide, 1)
    pick = iota(wide, 0) == me * 8 + (j >> 8) * 2 + ((j >> 3) & 1)
    picked = mm(counts, pick.astype(F32).astype(BF16))
    j = iota((N_CTX, CHUNKS * SPAN), 1)
    held = jnp.sum(
        jnp.where(iota((N_CTX, CHUNKS * SPAN), 0) == ((j >> 4) & 15), picked, 0.0), axis=0, keepdims=True
    )
    live = jnp.where((iota((1, CHUNKS * SPAN), 1) & 7).astype(F32) < held, 0.0, NEG)
    for c in range(CHUNKS):
        live_v[c] = live[:, c * SPAN : (c + 1) * SPAN]
    span = (SPAN, SPAN)
    si, sj = iota(span, 0), iota(span, 1)
    mask_v[...] = jnp.where((((si ^ sj) & 8) == 0) & (sj <= si), 0.0, NEG)

    @pl.loop(0, CHUNKS)
    def _(c):
        @pl.when(lead & (c == 1))
        def _():
            landed(bias_a_recv.at[pl.ds(0, N_CTX - 1)], small_rsem.at[1])
            bias_b[...] = jnp.sum(bias_a_recv[...], axis=0)
            bias_b_recv[my_head] = bias_b[...]
            pl.semaphore_wait(barrier, N_HEAD - 1)

            @pl.loop(1, N_HEAD)
            def _(step):
                pltpu.make_async_remote_copy(
                    bias_b, bias_b_recv.at[my_head], small_ssem.at[2], small_rsem.at[2],
                    device_id={"head": lax.rem(my_head + step, N_HEAD)}, device_id_type=MESH,
                ).start()

        landed(recv.at[c, pl.ds(0, N_CTX - 1)], recv_sem.at[c])
        q, k, v, g = (recv[c, :, a].reshape(SPAN, DIM) for a in range(4))
        out, dq, dk, dv, _ = attention(q, k, v, g, mask_v[...] + live_v[c])
        for a, r in enumerate((out, dq, dk, dv)):
            ret_send[c, :, a] = r.astype(BF16).reshape(N_CTX, ROWS, DIM)

        @pl.loop(1, N_CTX)
        def _(step):
            to = peer(step)
            pltpu.make_async_remote_copy(
                ret_send.at[c, to], ret_recv.at[c, me], rsend_sem.at[c], rrecv_sem.at[c],
                device_id={"ctx": to}, device_id_type=MESH,
            ).start()

        ret_recv[c, me] = ret_send[c, me]
        pick = (((iota((16, SPAN), 1) >> 3) & 1) == iota((16, SPAN), 0)).astype(F32).astype(BF16)
        sums = mm(pick, k)[0:2]
        o_cent[c] = sums / jnp.sqrt(jnp.mean(sums * sums, axis=-1, keepdims=True) + EPSILON)

    @pl.when(lead)
    def _():
        landed(bias_b_recv.at[pl.ds(0, N_HEAD - 1)], small_rsem.at[2])
        bias_c[...] = jnp.sum(bias_b_recv[...], axis=0)

        @pl.loop(1, N_CTX)
        def _(step):
            pltpu.make_async_remote_copy(
                bias_c, bias_d, small_ssem.at[3], small_rsem.at[3],
                device_id={"ctx": peer(step)}, device_id_type=MESH,
            ).start()

    for i in range(2):
        pltpu.make_async_remote_copy(
            grad_send.at[i], grad_recv.at[i], grad_ssem.at[i], grad_rsem.at[i],
            device_id={"ctx": behind}, device_id_type=MESH,
        ).wait_recv()
        wacc[i, pl.ds(TOK - WINDOW, WINDOW)] += grad_recv[i].astype(F32)
        (o_ldk, o_ldv)[i][...] = wacc[i].astype(BF16)
    acc[...] = jnp.zeros_like(acc)

    @pl.loop(0, CHUNKS)
    def _(c):
        landed(ret_recv.at[c, pl.ds(0, N_CTX - 1)], rrecv_sem.at[c])
        rows = jnp.concatenate([ret_recv[c, :, a].reshape(SPAN, DIM) for a in range(4)], axis=1)
        acc[...] += mm(back_hot[c], rows)

    for a, dst in enumerate((o_ro, o_rdq, o_rdk, o_rdv)):
        dst[...] = acc[:, a * DIM : (a + 1) * DIM].astype(BF16)

    for c in range(CHUNKS):
        part = send.at[c, pl.ds(0, N_CTX - 1)]
        pltpu.make_async_copy(part, part, send_sem.at[c]).wait()
        part = ret_send.at[c, pl.ds(0, N_CTX - 1)]
        pltpu.make_async_copy(part, part, rsend_sem.at[c]).wait()
    for i in range(2):
        pltpu.make_async_copy(halo.at[i], halo.at[i], halo_ssem.at[i]).wait()
        pltpu.make_async_copy(grad_send.at[i], grad_send.at[i], grad_ssem.at[i]).wait()
    landed(cnt_recv.at[pl.ds(0, N_CTX - 1)], small_ssem.at[0])

    @pl.when(lead)
    def _():
        o_bias[...] = bias_c[...]
        landed(bias_b_recv.at[pl.ds(0, N_HEAD - 1)], small_ssem.at[2])
        landed(bias_a_recv.at[pl.ds(0, N_CTX - 1)], small_ssem.at[3])

    @pl.when(me != 0)
    def _():
        landed(bias_d, small_rsem.at[3])
        o_bias[...] = bias_d[...]
        landed(bias_a, small_ssem.at[1])


def deliver(*refs):
    sources, targets, sems = refs[:10], refs[10:20], refs[20]
    copies = [pltpu.make_async_copy(s, t, sems.at[i]) for i, (s, t) in enumerate(zip(sources, targets))]
    for copy in copies:
        copy.start()
    for copy in copies:
        copy.wait()


def shards(rq, rk, rv, rg, lq, lk, lv, lg, clusters, cluster_slot, rel_bias):
    token_out = jax.ShapeDtypeStruct((TOK, DIM), BF16)
    vm = pltpu.VMEM
    dma = pltpu.SemaphoreType.DMA
    scratch = [
        vm((TOK, 4 * DIM), BF16),
        vm((TOK, DIM), BF16), vm((TOK, DIM), BF16), vm((TOK, DIM), BF16), vm((TOK, DIM), BF16),
        vm((CHUNKS, N_CTX, 4, ROWS, DIM), BF16), vm((CHUNKS, N_CTX, 4, ROWS, DIM), BF16),
        vm((CHUNKS, N_CTX, 4, ROWS, DIM), BF16), vm((CHUNKS, N_CTX, 4, ROWS, DIM), BF16),
        vm((2, WINDOW, DIM), BF16), vm((2, WINDOW, DIM), BF16), vm((2, WINDOW, DIM), BF16),
        vm((1, DIM), F32), vm((N_CTX, 1, DIM), F32),
        vm((1, DIM), F32), vm((N_CTX, 1, DIM), F32),
        vm((1, DIM), F32), vm((N_HEAD, 1, DIM), F32), vm((1, DIM), F32), vm((1, DIM), F32),
        vm((1, TOK), I32), vm((CHUNKS, TOK, SPAN), BF16), vm((CHUNKS, 1, SPAN), F32),
        vm((SPAN, SPAN), F32), vm((WINDOW, 2 * WINDOW), F32), vm((TOK, 4 * DIM), F32),
        vm((2, TOK, DIM), F32),
        vm((WINDOW, 2 * WINDOW), F32),
        dma((8,)),
        dma((CHUNKS,)), dma((CHUNKS,)), dma((CHUNKS,)), dma((CHUNKS,)),
        dma((2,)), dma((2,)), dma((2,)), dma((2,)), dma((4,)), dma((4,)), pltpu.SemaphoreType.REGULAR,
    ]
    anywhere = pl.BlockSpec(memory_space=pl.ANY)
    small = [jax.ShapeDtypeStruct((CHUNKS, 2, DIM), F32), jax.ShapeDtypeStruct((1, DIM), F32)]
    packed = pl.pallas_call(
        kernel,
        out_shape=[token_out] * 8 + small,
        in_specs=[anywhere] * 8 + [pl.BlockSpec(memory_space=pltpu.VMEM)] * 3,
        out_specs=[pl.BlockSpec(memory_space=pltpu.VMEM)] * 10,
        scratch_shapes=scratch,
        compiler_params=pltpu.CompilerParams(
            collective_id=0, has_side_effects=True, vmem_limit_bytes=VMEM_GRANT
        ),
        name="routing",
    )(rq, rk, rv, rg, lq, lk, lv, lg, clusters.reshape(4, 1, DIM), cluster_slot.reshape(1, 1, DIM), rel_bias.reshape(1, DIM))
    ro, rdq, rdk, rdv, lo, ldq, ldk, ldv, cent, bias = pl.pallas_call(
        deliver,
        out_shape=[token_out] * 8 + small,
        in_specs=[anywhere] * 10,
        out_specs=[anywhere] * 10,
        scratch_shapes=[dma((10,))],
        compiler_params=pltpu.CompilerParams(vmem_limit_bytes=VMEM_GRANT),
        name="deliver",
    )(*packed)
    return (
        ro, rdq, rdk, rdv, cent.reshape(1, 8, DIM), lo, ldq, ldk, ldv, bias.reshape(DIM),
    )


def solution(mesh):
    tokens = P("ctx", "head")
    return jax.shard_map(
        shards,
        mesh=mesh,
        in_specs=(tokens,) * 8 + (P("head", "ctx"), P("head", None), P()),
        out_specs=(tokens,) * 4 + (P("head", "ctx", None),) + (tokens,) * 4 + (P(),),
        check_vma=False,
    )
```

```python
import functools

import jax
import jax.numpy as jnp
from jax import lax
from jax.experimental import pallas as pl
from jax.experimental.pallas import tpu as pltpu
from jax.sharding import PartitionSpec as P

TOK = 512
DIM = 128
WINDOW = 128
N_CTX = 16
N_HEAD = 8
CHUNKS = 4
ROWS = 16
SPAN = N_CTX * ROWS
NEG = -1e30
FAR_CORNER = 10
EPSILON = 1e-06
VMEM_GRANT = 54140 * 1024
SCALE = DIM ** (-0.5)
F32 = jnp.float32
BF16 = jnp.bfloat16
I32 = jnp.int32
MESH = pl.DeviceIdType.MESH


def iota(shape, dim):
    return lax.broadcasted_iota(I32, shape, dim)


def mm(a, b):
    return jnp.dot(a, b, preferred_element_type=F32)


def mm_nt(a, b):
    return lax.dot_general(a, b, (((1,), (1,)), ((), ())), preferred_element_type=F32)


def mm_tn(a, b):
    return lax.dot_general(a, b, (((0,), (0,)), ((), ())), preferred_element_type=F32)


def landed(part, sem):
    pltpu.make_async_copy(part, part, sem).wait()


def attention(q, k, v, g, mask):
    scores = mm_nt(q, k) * SCALE + mask
    top = jnp.max(scores, axis=-1, keepdims=True)
    e = jnp.exp(scores - top)
    p = e / jnp.sum(e, axis=-1, keepdims=True)
    p_low = p.astype(BF16)
    dp = mm_nt(g, v)
    ds = p * (dp - jnp.sum(p * dp, axis=-1, keepdims=True))
    ds_low = ds.astype(BF16)
    out = mm(p_low, v)
    dq = mm(ds_low, k) * SCALE
    dk = mm_tn(ds_low, q) * SCALE
    dv = mm_tn(p_low, g)
    return out, dq, dk, dv, ds


def kernel(
    rq, rk, rv, rg, lq, lk, lv, lg, cl, slot, rb,
    o_ro, o_rdq, o_rdk, o_rdv, o_lo, o_ldq, o_ldk, o_ldv, o_cent, o_bias,
    tok, wq, wk, wv, wg,
    send, recv, ret_send, ret_recv, halo, grad_send, grad_recv,
    cnt_send, cnt_recv, bias_a, bias_a_recv, bias_b, bias_b_recv, bias_c, bias_d,
    flat_v, back_hot, live_v, mask_v, wbias, acc, wacc,
    bias_v,
    in_sem, send_sem, recv_sem, rsend_sem, rrecv_sem,
    halo_ssem, halo_rsem, grad_ssem, grad_rsem, small_ssem, small_rsem, go_sem,
):
    me = lax.axis_index("ctx")
    my_head = lax.axis_index("head")
    my_x = lax.rem(me, 4)
    my_y = lax.div(me, 4)
    ahead = lax.rem(me + 1, N_CTX)
    behind = lax.rem(me + N_CTX - 1, N_CTX)

    def peer(step):
        px = lax.rem(my_x + lax.rem(step, 4), 4)
        py = lax.rem(my_y + lax.div(step, 4), 4)
        return py * 4 + px

    lead = me == 0
    barrier = pltpu.get_barrier_semaphore()

    @pl.loop(0, N_CTX - 1)
    def _(i):
        to = peer(lax.rem(i + 9, N_CTX - 1) + 1)

        @pl.when(to != 0)
        def _():
            pl.semaphore_signal(barrier, inc=1, device_id={"ctx": to}, device_id_type=MESH)

    @pl.when(lead)
    def _():
        @pl.loop(1, N_HEAD)
        def _(step):
            pl.semaphore_signal(
                barrier, inc=1, device_id={"head": lax.rem(my_head + step, N_HEAD)}, device_id_type=MESH
            )

    def fetch(src, dst, i):
        copy = pltpu.make_async_copy(src, dst, in_sem.at[i])
        copy.start()
        return copy

    routed_in = [
        fetch(src, tok.at[:, pl.ds(i * DIM, DIM)], i) for i, src in enumerate((rq, rk, rv, rg))
    ]
    local_in = [fetch(src, dst, 4 + i) for i, (src, dst) in enumerate(((lk, wk), (lv, wv), (lq, wq), (lg, wg)))]

    cluster_rows = iota((DIM, TOK), 0)
    named = (jnp.concatenate([cl[i] for i in range(4)], axis=1) == cluster_rows).astype(F32).astype(BF16)
    slots16 = jnp.broadcast_to(slot[0].astype(F32), (16, DIM)).astype(BF16)
    slot_of = mm(slots16, named)[0:1].astype(I32)
    in_slot = slot_of == cluster_rows
    placed = in_slot.astype(F32).astype(BF16)
    upto = (iota((TOK, TOK), 0) <= iota((TOK, TOK), 1)).astype(F32).astype(BF16)
    ranks = mm(placed, upto)
    rank = jnp.sum(jnp.where(in_slot, ranks, 0.0), axis=0, keepdims=True).astype(I32) - 1
    flat = (
        ((slot_of >> 1) & 3) * SPAN + (slot_of >> 3) * ROWS + (slot_of & 1) * 8 + rank
    )
    flat_v[...] = flat
    cnt_send[...] = mm_nt(jnp.ones((16, TOK), BF16), placed)[0:1]

    for copy in routed_in:
        copy.wait()

    def pack(c):
        hot = (flat_v[...] == iota((SPAN, TOK), 0) + c * SPAN).astype(F32).astype(BF16)
        rows = mm(hot, tok[...]).astype(BF16)
        for a in range(4):
            send[c, :, a] = rows[:, a * DIM : (a + 1) * DIM].reshape(N_CTX, ROWS, DIM)

    pack(0)

    @pl.when(me != 0)
    def _():
        pl.semaphore_wait(barrier, N_CTX - 1)

    @pl.when(me == FAR_CORNER)
    def _():
        pl.semaphore_signal(go_sem, inc=1, device_id={"ctx": 0}, device_id_type=MESH)

    @pl.when(lead)
    def _():
        pl.semaphore_wait(go_sem, 1)


    for copy in local_in[:2]:
        copy.wait()
    for i, src in enumerate((wk, wv)):
        pltpu.make_async_remote_copy(
            src.at[pl.ds(TOK - WINDOW, WINDOW)], halo.at[i], halo_ssem.at[i], halo_rsem.at[i],
            device_id={"ctx": ahead}, device_id_type=MESH,
        ).start()

    cnt_recv[me] = cnt_send[...]

    @pl.loop(0, CHUNKS)
    def _(c):
        @pl.loop(1, N_CTX)
        def _(step):
            to = peer(step)
            pltpu.make_async_remote_copy(
                send.at[c, to], recv.at[c, me], send_sem.at[c], recv_sem.at[c],
                device_id={"ctx": to}, device_id_type=MESH,
            ).start()

        @pl.when(c == 0)
        def _():
            @pl.loop(1, N_CTX)
            def _(step):
                pltpu.make_async_remote_copy(
                    cnt_send, cnt_recv.at[me], small_ssem.at[0], small_rsem.at[0],
                    device_id={"ctx": peer(step)}, device_id_type=MESH,
                ).start()

        recv[c, me] = send[c, me]

        @pl.when(c < CHUNKS - 1)
        def _():
            pack(c + 1)

    back_hot[...] = jnp.zeros_like(back_hot)
    flat_col = jnp.transpose(jnp.broadcast_to(flat.astype(F32), (8, TOK)))[:, 0:1].astype(I32)

    @pl.loop(0, CHUNKS)
    def _(c):
        back_hot[c] = (flat_col == iota((TOK, SPAN), 1) + c * SPAN).astype(F32).astype(BF16)

    row_i = iota((WINDOW, 2 * WINDOW), 0)
    col_i = iota((WINDOW, 2 * WINDOW), 1)
    bias_col = jnp.sum(
        jnp.where(iota((DIM, DIM), 0) == iota((DIM, DIM), 1), rb[...], 0.0), axis=1, keepdims=True
    )
    spread = jnp.sum(jnp.where(row_i == WINDOW - col_i, bias_col, 0.0), axis=0, keepdims=True)
    spread = jnp.broadcast_to(spread, (WINDOW, 2 * WINDOW))
    for b in range(7):
        spread = jnp.where((row_i >> b) & 1 == 1, pltpu.roll(spread, 1 << b, 1), spread)
    offset = WINDOW + row_i - col_i
    wbias[...] = jnp.where((offset >= 0) & (offset < WINDOW), spread, NEG)

    for copy in local_in[2:]:
        copy.wait()

    def local_block(b, k, v, mask):
        rows = pl.ds(b * WINDOW, WINDOW)
        out, dq, dk, dv, ds = attention(wq[rows], k, v, wg[rows], mask)
        o_lo[rows] = out.astype(BF16)
        o_ldq[rows] = dq.astype(BF16)
        return dk, dv, ds

    wacc[...] = jnp.zeros_like(wacc)
    bias_v[...] = jnp.zeros_like(bias_v)

    @pl.loop(1, 4)
    def _(b):
        at = pl.multiple_of((b - 1) * WINDOW, WINDOW)
        frame = pl.ds(at, 2 * WINDOW)
        dk, dv, ds = local_block(b, wk[frame], wv[frame], wbias[...])
        wacc[0, frame] += dk
        wacc[1, frame] += dv
        bias_v[...] += ds

    for i in range(2):
        pltpu.make_async_remote_copy(
            wk.at[pl.ds(0, WINDOW)], halo.at[i], halo_ssem.at[i], halo_rsem.at[i],
            device_id={"ctx": ahead}, device_id_type=MESH,
        ).wait_recv()
    first = jnp.where((col_i < WINDOW) & (me == 0), NEG, wbias[...])
    own = pl.ds(0, WINDOW)
    dk, dv, ds = local_block(
        0,
        jnp.concatenate([halo[0], wk[own]], axis=0),
        jnp.concatenate([halo[1], wv[own]], axis=0),
        first,
    )
    for i, d in enumerate((dk, dv)):
        grad_send[i] = d[:WINDOW].astype(BF16)
        wacc[i, own] += d[WINDOW:]
        pltpu.make_async_remote_copy(
            grad_send.at[i], grad_recv.at[i], grad_ssem.at[i], grad_rsem.at[i],
            device_id={"ctx": behind}, device_id_type=MESH,
        ).start()

    total = bias_v[...] + ds
    for b in range(7):
        total = jnp.where((row_i >> b) & 1 == 1, pltpu.roll(total, 2 * WINDOW - (1 << b), 1), total)
    by_col = jnp.sum(total, axis=0, keepdims=True)
    square = (2 * WINDOW, 2 * WINDOW)
    by_row = jnp.sum(jnp.where(iota(square, 0) == iota(square, 1), by_col, 0.0), axis=1, keepdims=True)
    tall = (2 * WINDOW, WINDOW)
    bias_a[...] = jnp.sum(
        jnp.where(iota(tall, 0) == WINDOW - iota(tall, 1), by_row, 0.0), axis=0, keepdims=True
    )

    @pl.when(me != 0)
    def _():
        pltpu.make_async_remote_copy(
            bias_a, bias_a_recv.at[me], small_ssem.at[1], small_rsem.at[1],
            device_id={"ctx": 0}, device_id_type=MESH,
        ).start()

    @pl.when(lead)
    def _():
        bias_a_recv[0] = bias_a[...]

    landed(cnt_recv.at[pl.ds(0, N_CTX - 1)], small_rsem.at[0])
    counts = jnp.concatenate([cnt_recv[s] for s in range(N_CTX)], axis=0).astype(BF16)
    wide = (DIM, CHUNKS * SPAN)
    j = iota(wide, 1)
    pick = iota(wide, 0) == me * 8 + (j >> 8) * 2 + ((j >> 3) & 1)
    picked = mm(counts, pick.astype(F32).astype(BF16))
    j = iota((N_CTX, CHUNKS * SPAN), 1)
    held = jnp.sum(
        jnp.where(iota((N_CTX, CHUNKS * SPAN), 0) == ((j >> 4) & 15), picked, 0.0), axis=0, keepdims=True
    )
    live = jnp.where((iota((1, CHUNKS * SPAN), 1) & 7).astype(F32) < held, 0.0, NEG)
    for c in range(CHUNKS):
        live_v[c] = live[:, c * SPAN : (c + 1) * SPAN]
    span = (SPAN, SPAN)
    si, sj = iota(span, 0), iota(span, 1)
    mask_v[...] = jnp.where((((si ^ sj) & 8) == 0) & (sj <= si), 0.0, NEG)

    @pl.loop(0, CHUNKS)
    def _(c):
        @pl.when(lead & (c == 1))
        def _():
            landed(bias_a_recv.at[pl.ds(0, N_CTX - 1)], small_rsem.at[1])
            bias_b[...] = jnp.sum(bias_a_recv[...], axis=0)
            bias_b_recv[my_head] = bias_b[...]
            pl.semaphore_wait(barrier, N_HEAD - 1)

            @pl.loop(1, N_HEAD)
            def _(step):
                pltpu.make_async_remote_copy(
                    bias_b, bias_b_recv.at[my_head], small_ssem.at[2], small_rsem.at[2],
                    device_id={"head": lax.rem(my_head + step, N_HEAD)}, device_id_type=MESH,
                ).start()

        landed(recv.at[c, pl.ds(0, N_CTX - 1)], recv_sem.at[c])
        q, k, v, g = (recv[c, :, a].reshape(SPAN, DIM) for a in range(4))
        out, dq, dk, dv, _ = attention(q, k, v, g, mask_v[...] + live_v[c])
        for a, r in enumerate((out, dq, dk, dv)):
            ret_send[c, :, a] = r.astype(BF16).reshape(N_CTX, ROWS, DIM)

        @pl.loop(1, N_CTX)
        def _(step):
            to = peer(step)
            pltpu.make_async_remote_copy(
                ret_send.at[c, to], ret_recv.at[c, me], rsend_sem.at[c], rrecv_sem.at[c],
                device_id={"ctx": to}, device_id_type=MESH,
            ).start()

        ret_recv[c, me] = ret_send[c, me]
        pick = (((iota((16, SPAN), 1) >> 3) & 1) == iota((16, SPAN), 0)).astype(F32).astype(BF16)
        sums = mm(pick, k)[0:2]
        o_cent[c] = sums / jnp.sqrt(jnp.mean(sums * sums, axis=-1, keepdims=True) + EPSILON)

    @pl.when(lead)
    def _():
        landed(bias_b_recv.at[pl.ds(0, N_HEAD - 1)], small_rsem.at[2])
        bias_c[...] = jnp.sum(bias_b_recv[...], axis=0)

        @pl.loop(1, N_CTX)
        def _(step):
            pltpu.make_async_remote_copy(
                bias_c, bias_d, small_ssem.at[3], small_rsem.at[3],
                device_id={"ctx": peer(step)}, device_id_type=MESH,
            ).start()

    for i in range(2):
        pltpu.make_async_remote_copy(
            grad_send.at[i], grad_recv.at[i], grad_ssem.at[i], grad_rsem.at[i],
            device_id={"ctx": behind}, device_id_type=MESH,
        ).wait_recv()
        wacc[i, pl.ds(TOK - WINDOW, WINDOW)] += grad_recv[i].astype(F32)
        (o_ldk, o_ldv)[i][...] = wacc[i].astype(BF16)
    acc[...] = jnp.zeros_like(acc)

    @pl.loop(0, CHUNKS)
    def _(c):
        landed(ret_recv.at[c, pl.ds(0, N_CTX - 1)], rrecv_sem.at[c])
        rows = jnp.concatenate([ret_recv[c, :, a].reshape(SPAN, DIM) for a in range(4)], axis=1)
        acc[...] += mm(back_hot[c], rows)

    for a, dst in enumerate((o_ro, o_rdq, o_rdk, o_rdv)):
        dst[...] = acc[:, a * DIM : (a + 1) * DIM].astype(BF16)

    for c in range(CHUNKS):
        part = send.at[c, pl.ds(0, N_CTX - 1)]
        pltpu.make_async_copy(part, part, send_sem.at[c]).wait()
        part = ret_send.at[c, pl.ds(0, N_CTX - 1)]
        pltpu.make_async_copy(part, part, rsend_sem.at[c]).wait()
    for i in range(2):
        pltpu.make_async_copy(halo.at[i], halo.at[i], halo_ssem.at[i]).wait()
        pltpu.make_async_copy(grad_send.at[i], grad_send.at[i], grad_ssem.at[i]).wait()
    landed(cnt_recv.at[pl.ds(0, N_CTX - 1)], small_ssem.at[0])

    @pl.when(lead)
    def _():
        o_bias[...] = bias_c[...]
        landed(bias_b_recv.at[pl.ds(0, N_HEAD - 1)], small_ssem.at[2])
        landed(bias_a_recv.at[pl.ds(0, N_CTX - 1)], small_ssem.at[3])

    @pl.when(me != 0)
    def _():
        landed(bias_d, small_rsem.at[3])
        o_bias[...] = bias_d[...]
        landed(bias_a, small_ssem.at[1])


def deliver(*refs):
    sources, targets, sems = refs[:10], refs[10:20], refs[20]
    copies = [pltpu.make_async_copy(s, t, sems.at[i]) for i, (s, t) in enumerate(zip(sources, targets))]
    for copy in copies:
        copy.start()
    for copy in copies:
        copy.wait()


def shards(rq, rk, rv, rg, lq, lk, lv, lg, clusters, cluster_slot, rel_bias):
    token_out = jax.ShapeDtypeStruct((TOK, DIM), BF16)
    vm = pltpu.VMEM
    dma = pltpu.SemaphoreType.DMA
    scratch = [
        vm((TOK, 4 * DIM), BF16),
        vm((TOK, DIM), BF16), vm((TOK, DIM), BF16), vm((TOK, DIM), BF16), vm((TOK, DIM), BF16),
        vm((CHUNKS, N_CTX, 4, ROWS, DIM), BF16), vm((CHUNKS, N_CTX, 4, ROWS, DIM), BF16),
        vm((CHUNKS, N_CTX, 4, ROWS, DIM), BF16), vm((CHUNKS, N_CTX, 4, ROWS, DIM), BF16),
        vm((2, WINDOW, DIM), BF16), vm((2, WINDOW, DIM), BF16), vm((2, WINDOW, DIM), BF16),
        vm((1, DIM), F32), vm((N_CTX, 1, DIM), F32),
        vm((1, DIM), F32), vm((N_CTX, 1, DIM), F32),
        vm((1, DIM), F32), vm((N_HEAD, 1, DIM), F32), vm((1, DIM), F32), vm((1, DIM), F32),
        vm((1, TOK), I32), vm((CHUNKS, TOK, SPAN), BF16), vm((CHUNKS, 1, SPAN), F32),
        vm((SPAN, SPAN), F32), vm((WINDOW, 2 * WINDOW), F32), vm((TOK, 4 * DIM), F32),
        vm((2, TOK, DIM), F32),
        vm((WINDOW, 2 * WINDOW), F32),
        dma((8,)),
        dma((CHUNKS,)), dma((CHUNKS,)), dma((CHUNKS,)), dma((CHUNKS,)),
        dma((2,)), dma((2,)), dma((2,)), dma((2,)), dma((4,)), dma((4,)), pltpu.SemaphoreType.REGULAR,
    ]
    anywhere = pl.BlockSpec(memory_space=pl.ANY)
    small = [jax.ShapeDtypeStruct((CHUNKS, 2, DIM), F32), jax.ShapeDtypeStruct((1, DIM), F32)]
    packed = pl.pallas_call(
        kernel,
        out_shape=[token_out] * 8 + small,
        in_specs=[anywhere] * 8 + [pl.BlockSpec(memory_space=pltpu.VMEM)] * 3,
        out_specs=[pl.BlockSpec(memory_space=pltpu.VMEM)] * 10,
        scratch_shapes=scratch,
        compiler_params=pltpu.CompilerParams(
            collective_id=0, has_side_effects=True, vmem_limit_bytes=VMEM_GRANT
        ),
        name="routing",
    )(rq, rk, rv, rg, lq, lk, lv, lg, clusters.reshape(4, 1, DIM), cluster_slot.reshape(1, 1, DIM), rel_bias.reshape(1, DIM))
    ro, rdq, rdk, rdv, lo, ldq, ldk, ldv, cent, bias = pl.pallas_call(
        deliver,
        out_shape=[token_out] * 8 + small,
        in_specs=[anywhere] * 10,
        out_specs=[anywhere] * 10,
        scratch_shapes=[dma((10,))],
        compiler_params=pltpu.CompilerParams(vmem_limit_bytes=VMEM_GRANT),
        name="deliver",
    )(*packed)
    return (
        ro, rdq, rdk, rdv, cent.reshape(1, 8, DIM), lo, ldq, ldk, ldv, bias.reshape(DIM),
    )


def solution(mesh):
    tokens = P("ctx", "head")
    return jax.shard_map(
        shards,
        mesh=mesh,
        in_specs=(tokens,) * 8 + (P("head", "ctx"), P("head", None), P()),
        out_specs=(tokens,) * 4 + (P("head", "ctx", None),) + (tokens,) * 4 + (P(),),
        check_vma=False,
    )
```
